32 devices in a mesh: slab: 8 (over y, x, core), pencil: 4 (over z).
Axes of the slice: x: 2, y: 2, z: 4, core: 2. Of those that a mesh axis runs over, the one named last changes fastest.
Arguments:
- orbitals: float32 [4, 192, 192, 192], P(None, 'slab', 'pencil'), may hold values from -6 to 6
- potential: float32 [192, 192, 192], P('slab', 'pencil'), may hold values from 0.5 to 2.5
- unlocked: int32 [4], replicated, may hold values 0 or 1
Outputs:
- orthonormal: float32 [4, 192, 192, 192], P(None, 'slab', 'pencil')
The draws below stay inside these ranges and needn't reach their ends.
Inputs may be any that keep to these rules, and one draw needn't show every extreme that they name: `unlocked`: 1 marks a band that is filtered, 0 a locked band kept as it is.
All inputs are finite; a program needn't handle non-finite values.
Results may differ from the reference program's by a relative error of at most 0.00005.
Values sent between devices are 32-bit elements; how exact they have to be, the bound alone decides.
A program may use at most 128 MiB of HBM per device.

```python
import jax
import jax.numpy as jnp
from jax import lax

NG = 192
NB = 4


def draw_orbitals(key, part):
    weight_key = jax.random.fold_in(key, 11)
    common_key = jax.random.fold_in(key, 12)
    private_key = jax.random.fold_in(key, 13)
    weights = jax.random.uniform(weight_key, (NB,), jnp.float32, 0.5, 0.9)
    common = jax.random.normal(common_key, (NG, NG, NG), jnp.float32)
    private = jax.random.normal(private_key, (NB, NG, NG, NG), jnp.float32)
    values = weights[:, None, None, None] * common[None] + private
    return jnp.clip(values, -6.0, 6.0).astype(jnp.float32)


def plant(drawn, rng, smallest, largest):
    shape = drawn.shape
    place = [jax.random.randint(jax.random.fold_in(rng, axis), (), 0, shape[axis]) for axis in range(len(shape))]
    drawn = drawn.at[tuple(place)].set(smallest)
    longest = shape.index(max(shape))
    place[longest] = (place[longest] + 1) % shape[longest]
    return drawn.at[tuple(place)].set(largest)


def level_of(key, extent, shards, least, top_value):
    level = 1.0
    for dim, blocks in shards:
        heights = jax.random.uniform(jax.random.fold_in(jax.random.fold_in(key, 6), dim), (blocks,), jnp.float32, least / len(shards), top_value / len(shards))
        level = level * jnp.repeat(jnp.exp(heights), extent[dim] // blocks).reshape((-1,) + (1,) * (len(extent) - 1 - dim))
    return level


def setup_inputs(seed: int = 0) -> dict:
    keys = jax.random.split(jax.random.key(seed), 4)
    return {
        "orbitals": draw_orbitals(jax.random.fold_in(keys[3], 71), 0),
        "potential": jnp.clip(0.5 + 2.0 * jax.random.uniform(keys[1], (NG, NG, NG), jnp.float32) ** level_of(keys[1], (NG, NG, NG), ((0, 8), (1, 4)), -0.2, 0.2), 0.5, 2.5),
        "unlocked": plant((jax.random.randint(keys[2], (NB,), 0, 4) < 3).astype(jnp.int32), jax.random.fold_in(keys[2], 1), 0, 1),
    }


kinetic_scale = 4.0
filter_center = 1.0
filter_half = 1.5

def kinetic_table():
    index = jnp.arange(NG)
    modes = jnp.where(index < NG // 2, index, index - NG).astype(jnp.float32)
    squared = modes[:, None, None] ** 2 + modes[None, :, None] ** 2 + modes[None, None, :] ** 2
    radius = float((NG // 4) ** 2)
    return jnp.where(squared < radius, kinetic_scale * squared / radius, 0.0)

def reference(orbitals, potential, unlocked):
    kinetic = kinetic_table().astype(orbitals.dtype)

    def apply_one(orbital):
        spectrum = jnp.fft.fftn(orbital)
        kinetic_part = jnp.real(jnp.fft.ifftn(spectrum * kinetic)).astype(orbital.dtype)
        return kinetic_part + potential * orbital
    applied = lax.map(apply_one, orbitals)
    filtered = jnp.where(unlocked[:, None, None, None] == 1, (applied - filter_center * orbitals) / filter_half, orbitals)
    flattened = filtered.reshape(NB, -1)
    intersection = jnp.dot(flattened, flattened.T, precision=lax.Precision.HIGHEST) / float(NG ** 3)
    factor = jnp.linalg.cholesky(intersection)
    result = jax.scipy.linalg.solve_triangular(factor, flattened, lower=True)
    return result.reshape(orbitals.shape)
```

```python
import functools
import math

import jax
import jax.numpy as jnp
import numpy as np
from jax import lax
from jax.experimental import pallas as pl
from jax.experimental.pallas import tpu as pltpu
from jax.sharding import PartitionSpec as P

MESH = pl.DeviceIdType.MESH


def dft_tables(length, slabs, pencils, chunks):
    half = length // 4
    pair = half // (slabs * chunks)
    place = np.arange(length)
    modes = np.arange(2 * half) - half
    third = np.arange(half)

    def waves(mode):
        angle = 2.0 * np.pi / length * ((mode[:, None] * place[None, :]) % length)
        return np.cos(angle), np.sin(angle)

    cos_k, sin_k = waves(third)
    weight = np.where(third == 0, 1.0, 2.0)[:, None]

    def order(cosine, sine):
        both = np.stack([cosine, sine], 0).reshape(2, chunks, slabs, pair, length)
        return both.transpose(1, 2, 0, 3, 4).reshape(2 * half, length)

    forward_x = order(cos_k, -sin_k)
    inverse_x = order(weight * cos_k, -weight * sin_k)
    cosine, sine = waves(modes)
    forward = np.stack([np.stack([cosine, sine], 1), np.stack([-sine, cosine], 1)], 0)
    inverse = np.stack([np.stack([cosine.T, -sine.T], 1), np.stack([sine.T, cosine.T], 1)], 0)
    f_block = 2 * half // pencils
    a_block = length // slabs
    c_block = length // pencils
    forward_a = forward.reshape(2, pencils, f_block, 2 * length).transpose(1, 0, 2, 3).reshape(4 * half, 2 * length)
    forward_c = forward.reshape(4 * half, 2 * length).T
    inverse_c = inverse.reshape(2, pencils, c_block, 4 * half).transpose(1, 0, 2, 3).reshape(2 * length, 4 * half).T
    inverse_a = inverse.reshape(2, slabs, a_block, 4 * half).transpose(1, 0, 2, 3).reshape(2 * length, 4 * half)
    tables = (forward_x, forward_a, forward_c, inverse_c, inverse_a, inverse_x)
    return [np.ascontiguousarray(t, dtype=np.float32) for t in tables]


def matmul(left, right, contract=((1,), (0,))):
    return lax.dot_general(
        left, right, (contract, ((), ())), precision=lax.Precision.HIGHEST, preferred_element_type=jnp.float32
    )


def kernel(sizes, unlocked, orbitals, potential, fx, fa, fc, ic, ia, ix, row_k, row_f, col_s, out,
           lines, s1, r1, s2, r2, s3, r3, s4, r4, back, sums, g1, h1, g2, h2,
           own, send1, recv1, send2, recv2, send3, recv3, send4, recv4, gs1, gr1, gs2, gr2):
    slabs, pencils, chunks, pair, bands, length = sizes
    rows_a = orbitals.shape[1]
    rows_c = orbitals.shape[2]
    half = length // 4
    f_block = 2 * half // pencils
    wide = bands * rows_c
    i_s = lax.axis_index("slab")
    i_p = lax.axis_index("pencil")

    def slab_peer(d):
        return lax.rem(i_s + d, slabs)

    def pencil_peer(d):
        return lax.rem(i_p + d, pencils)

    barrier = pltpu.get_barrier_semaphore()
    for d in range(1, slabs):
        pl.semaphore_signal(barrier, inc=1, device_id=(slab_peer(d), i_p), device_id_type=MESH)
    for d in range(1, pencils):
        pl.semaphore_signal(barrier, inc=1, device_id=(i_s, pencil_peer(d)), device_id_type=MESH)

    def to_slab(d, src, dst, send, recv):
        return pltpu.make_async_remote_copy(
            src_ref=src, dst_ref=dst, send_sem=send, recv_sem=recv,
            device_id=(slab_peer(d), i_p), device_id_type=MESH)

    def to_pencil(d, src, dst, send, recv):
        return pltpu.make_async_remote_copy(
            src_ref=src, dst_ref=dst, send_sem=send, recv_sem=recv,
            device_id=(i_s, pencil_peer(d)), device_id_type=MESH)

    mine_a = pl.ds(pl.multiple_of(i_s * rows_a, 8), rows_a)
    mine_f = pl.ds(pl.multiple_of(i_p * f_block, 8), f_block)

    def copies(which, q):
        if which == 0:
            remote = [to_slab(d, s1.at[q, slab_peer(d)], r1.at[q, :, mine_a, :], send1.at[q, d], recv1.at[q, d])
                      for d in range(1, slabs)]
            local = pltpu.make_async_copy(s1.at[q, i_s], r1.at[q, :, mine_a, :], own.at[0, q])
        elif which == 1:
            remote = [to_pencil(d, s2.at[q, pencil_peer(d)], r2.at[q, i_p], send2.at[q, d], recv2.at[q, d])
                      for d in range(1, pencils)]
            local = pltpu.make_async_copy(s2.at[q, i_p], r2.at[q, i_p], own.at[1, q])
        elif which == 2:
            remote = [to_pencil(d, s3.at[q, pencil_peer(d)], r3.at[q, :, mine_f, :], send3.at[q, d], recv3.at[q, d])
                      for d in range(1, pencils)]
            local = pltpu.make_async_copy(s3.at[q, i_p], r3.at[q, :, mine_f, :], own.at[2, q])
        else:
            remote = [to_slab(d, s4.at[q, slab_peer(d)], r4.at[q, i_s], send4.at[q, d], recv4.at[q, d])
                      for d in range(1, slabs)]
            local = pltpu.make_async_copy(s4.at[q, i_s], r4.at[q, i_s], own.at[3, q])
        return remote, local

    def start(which, q):
        remote, local = copies(which, q)
        for copy in remote:
            copy.start()
        local.start()

    def arrived(which, q):
        remote, local = copies(which, q)
        for copy in remote:
            copy.wait_recv()
        local.wait()

    modes_x = 2 * half

    def forward_line(a, carry):
        rows = orbitals[:, pl.ds(a, 1)].reshape(wide, length)
        result = matmul(fx[...], rows, ((1,), (1,)))
        at = pl.multiple_of(a * modes_x, modes_x)
        for t in range(lines.shape[0]):
            low, high = t * 128, min(t * 128 + 128, wide)
            lines[t, pl.ds(at, modes_x), 0:high - low] = result[:, low:high]
        return carry

    lax.fori_loop(0, rows_a, forward_line, 0)
    pl.semaphore_wait(barrier, slabs - 1 + pencils - 1)

    def line_rows(ref, i):
        parts = []
        for t in range(ref.shape[0]):
            size = min(128, wide - t * 128)
            parts.append(ref[t, pl.ds(i, rows_a, stride=modes_x), :][:, :size])
        return parts

    for q in range(chunks):
        for j in range(slabs):
            for r in range(2):
                parts = []
                for k in range(pair):
                    parts += line_rows(lines, ((q * slabs + j) * 2 + r) * pair + k)
                s1[q, j, r] = jnp.concatenate(parts, 1)
        start(0, q)

    packed = pair * wide
    for q in range(chunks):
        arrived(0, q)
        result = matmul(fa[...], r1[q].reshape(2 * length, packed))
        s2[q] = result.reshape(pencils, 2, f_block, packed)
        start(1, q)

    for q in range(chunks):
        arrived(1, q)
        blocks = []
        for kb in range(pair * bands):
            lanes = slice(kb * rows_c, (kb + 1) * rows_c)
            blocks.append(jnp.concatenate([r2[q, p, r, :, lanes] for r in range(2) for p in range(pencils)], 1))
        spectrum = matmul(jnp.concatenate(blocks, 0), fc[...])
        mode_k = row_k[...] + (q * slabs * pair + i_s * pair).astype(jnp.float32)
        mode_f = row_f[...] + (i_p * f_block - half).astype(jnp.float32)
        squared = mode_k * mode_k + mode_f * mode_f + col_s[...]
        radius = float(half * half)
        kinetic = jnp.where(squared < radius, 4.0 * squared / radius, 0.0) * (1.0 / float(length**3))
        result = matmul(spectrum * kinetic, ic[...])
        for p in range(pencils):
            for r in range(2):
                lanes = slice((p * 2 + r) * rows_c, (p * 2 + r + 1) * rows_c)
                s3[q, p, r] = jnp.concatenate(
                    [result[kb * f_block:(kb + 1) * f_block, lanes] for kb in range(pair * bands)], 1)
        start(2, q)

    for q in range(chunks):
        arrived(2, q)
        result = matmul(ia[...], r3[q].reshape(4 * half, packed))
        s4[q] = result.reshape(slabs, 2, rows_a, packed)
        start(3, q)

    for q in range(chunks):
        arrived(3, q)
        for j in range(slabs):
            for r in range(2):
                value = r4[q, j, r]
                for k in range(pair):
                    i = ((q * slabs + j) * 2 + r) * pair + k
                    for t in range(back.shape[0]):
                        low, high = t * 128, min(t * 128 + 128, wide)
                        piece = value[:, k * wide + low:k * wide + high]
                        if high - low < 128:
                            piece = jnp.concatenate([piece, jnp.zeros((rows_a, 128 - high + low), jnp.float32)], 1)
                        back[t, pl.ds(i, rows_a, stride=modes_x), :] = piece

    sums[...] = jnp.zeros_like(sums)

    def inverse_line(a, carry):
        at = pl.multiple_of(a * modes_x, modes_x)
        spectrum = jnp.concatenate(
            [back[t, pl.ds(at, modes_x), 0:min(128, wide - t * 128)] for t in range(back.shape[0])], 1)
        kinetic_part = matmul(spectrum, ix[...], ((0,), (0,)))
        level = potential[pl.ds(a, 1)].reshape(rows_c, length)
        filtered = []
        for b in range(bands):
            orbital = orbitals[b, pl.ds(a, 1)].reshape(rows_c, length)
            applied = kinetic_part[b * rows_c:(b + 1) * rows_c] + level * orbital
            value = jnp.where(unlocked[b] == 1, (applied - orbital) / 1.5, orbital)
            out[b, pl.ds(a, 1)] = value.reshape(1, rows_c, length)
            filtered.append(value)
        n = 0
        for b in range(bands):
            for e in range(b + 1):
                product = filtered[b] * filtered[e]
                sums[n] += product.reshape(rows_c // 8, 8, length).sum(0)
                n += 1
        return carry

    lax.fori_loop(0, rows_a, inverse_line, 0)

    total = jnp.sum(jnp.sum(sums[...], axis=1), axis=1, keepdims=True)
    g1[...] = jnp.broadcast_to(total, g1.shape)
    shares = [to_slab(d, g1, h1.at[i_s], gs1.at[d], gr1.at[d]) for d in range(1, slabs)]
    for copy in shares:
        copy.start()
    h1[pl.ds(i_s, 1)] = g1[...][None]
    for copy in shares:
        copy.wait()
    g2[...] = jnp.sum(h1[...], axis=0)
    shares = [to_pencil(d, g2, h2.at[i_p], gs2.at[d], gr2.at[d]) for d in range(1, pencils)]
    for copy in shares:
        copy.start()
    h2[pl.ds(i_p, 1)] = g2[...][None]
    for copy in shares:
        copy.wait()
    gram = jnp.sum(h2[...], axis=0) / float(length**3)

    factor = {}
    for b in range(bands):
        for e in range(b + 1):
            n = b * (b + 1) // 2 + e
            value = gram[n:n + 1, 0:1]
            for m in range(e):
                value = value - factor[b, m] * factor[e, m]
            factor[b, e] = jnp.sqrt(value) if b == e else value / factor[e, e]
    inverse = [1.0 / factor[b, b] for b in range(bands)]

    def solve_line(a, carry):
        solved = []
        for b in range(bands):
            value = out[b, pl.ds(a, 1)].reshape(rows_c, length)
            for m in range(b):
                value = value - factor[b, m] * solved[m]
            value = value * inverse[b]
            out[b, pl.ds(a, 1)] = value.reshape(1, rows_c, length)
            solved.append(value)
        return carry

    lax.fori_loop(0, rows_a, solve_line, 0)
    for which in range(4):
        for q in range(chunks):
            for copy in copies(which, q)[0]:
                copy.wait_send()


def by_kernel(slabs, pencils, chunks, orbitals, potential, unlocked):
    bands, rows_a, rows_c, length = orbitals.shape
    half = length // 4
    pair = half // (slabs * chunks)
    f_block = 2 * half // pencils
    wide = bands * rows_c
    packed = pair * wide
    tiles = -(-wide // 128)
    pairs = bands * (bands + 1) // 2
    tables = dft_tables(length, slabs, pencils, chunks)
    rows = np.arange(pair * bands * f_block)
    row_k = (rows // (bands * f_block)).astype(np.float32)[:, None]
    row_f = (rows % f_block).astype(np.float32)[:, None]
    col_s = ((np.arange(4 * half) % (2 * half) - half).astype(np.float32) ** 2)[None, :]
    vmem = pl.BlockSpec(memory_space=pltpu.VMEM)
    f32 = jnp.float32
    dma = pltpu.SemaphoreType.DMA
    scratch = [
        pltpu.VMEM((tiles, rows_a * 2 * half, 128), f32),
        pltpu.VMEM((chunks, slabs, 2, rows_a, packed), f32),
        pltpu.VMEM((chunks, 2, length, packed), f32),
        pltpu.VMEM((chunks, pencils, 2, f_block, packed), f32),
        pltpu.VMEM((chunks, pencils, 2, f_block, packed), f32),
        pltpu.VMEM((chunks, pencils, 2, f_block, packed), f32),
        pltpu.VMEM((chunks, 2, 2 * half, packed), f32),
        pltpu.VMEM((chunks, slabs, 2, rows_a, packed), f32),
        pltpu.VMEM((chunks, slabs, 2, rows_a, packed), f32),
        pltpu.VMEM((tiles, rows_a * 2 * half, 128), f32),
        pltpu.VMEM((pairs, 8, length), f32),
        pltpu.VMEM((pairs, 128), f32),
        pltpu.VMEM((slabs, pairs, 128), f32),
        pltpu.VMEM((pairs, 128), f32),
        pltpu.VMEM((pencils, pairs, 128), f32),
        dma((4, chunks)),
        dma((chunks, slabs)), dma((chunks, slabs)),
        dma((chunks, pencils)), dma((chunks, pencils)),
        dma((chunks, pencils)), dma((chunks, pencils)),
        dma((chunks, slabs)), dma((chunks, slabs)),
        dma((slabs,)), dma((slabs,)),
        dma((pencils,)), dma((pencils,)),
    ]
    flops = 2 * rows_a * wide * length * 2 * half * 6
    return pl.pallas_call(
        functools.partial(kernel, (slabs, pencils, chunks, pair, bands, length)),
        out_shape=jax.ShapeDtypeStruct(orbitals.shape, f32),
        in_specs=[pl.BlockSpec(memory_space=pltpu.SMEM)] + [vmem] * 11,
        out_specs=vmem,
        scratch_shapes=scratch,
        compiler_params=pltpu.CompilerParams(
            collective_id=0, has_side_effects=True, vmem_limit_bytes=56 * 1024 * 1024),
        cost_estimate=pl.CostEstimate(flops=flops, bytes_accessed=10 * 2**20, transcendentals=0),
    )(unlocked, orbitals, potential, *[jnp.asarray(t) for t in tables],
      jnp.asarray(row_k), jnp.asarray(row_f), jnp.asarray(col_s))


NG = 192


kinetic_scale = 4.0
filter_center = 1.0
filter_half = 1.5
highest = lax.Precision.HIGHEST


def frequencies(number, length):
    index = jnp.arange(number, dtype=jnp.int32)
    if number == length:
        return jnp.where(index < length // 2, index, index - length)
    return index - length // 4


def tables(number, length):
    modes = frequencies(number, length)
    places = jnp.arange(length, dtype=jnp.int32)
    product = places[:, None] * modes[None, :] % length
    angle = 2.0 * math.pi / length * product.astype(jnp.float32)
    return (jnp.cos(angle), jnp.sin(angle))


def forward_table(cosine, sine):
    return jnp.stack([jnp.stack([cosine, -sine], 1), jnp.stack([sine, cosine], 1)], 1)


def inverse_table(cosine, sine):
    cos_t = cosine.T
    sin_t = sine.T
    return jnp.stack([jnp.stack([cos_t, sin_t], 1), jnp.stack([-sin_t, cos_t], 1)], 1)


def by_collectives(orbitals, potential, unlocked):
    length = orbitals.shape[3]
    kept_modes = length // 2
    cos_k, sin_k = tables(kept_modes, length)
    cos_f, sin_f = tables(length, length)
    first_forward = jnp.stack([cos_k, -sin_k], 1)
    first_inverse = jnp.stack([cos_k.T, -sin_k.T], 1)
    second_forward = forward_table(cos_k, sin_k)
    second_inverse = inverse_table(cos_k, sin_k)
    depth_forward = forward_table(cos_f, sin_f)
    depth_inverse = inverse_table(cos_f, sin_f)
    pencil_block = kept_modes // lax.axis_size("pencil")
    slab_block = kept_modes // lax.axis_size("slab")
    kept_list = frequencies(kept_modes, length)
    third_modes = lax.dynamic_slice_in_dim(
        kept_list, lax.axis_index("pencil") * pencil_block, pencil_block
    ).astype(jnp.float32)
    second_modes = lax.dynamic_slice_in_dim(
        kept_list, lax.axis_index("slab") * slab_block, slab_block
    ).astype(jnp.float32)
    first_modes = frequencies(length, length).astype(jnp.float32)
    squared = (
        third_modes[:, None, None] ** 2
        + second_modes[None, :, None] ** 2
        + first_modes[None, None, :] ** 2
    )
    radius = float((length // 4) ** 2)
    kinetic = jnp.where(squared < radius, kinetic_scale * squared / radius, 0.0)
    lines_k = jnp.einsum("bacx,xrk->bacrk", orbitals, first_forward, precision=highest)
    along_f = jnp.einsum(
        "bacrk,crsf->baksf",
        lax.all_to_all(lines_k, "pencil", split_axis=4, concat_axis=2, tiled=True),
        second_forward,
        precision=highest,
    )
    spectra = jnp.einsum(
        "baksf,astg->bkftg",
        lax.all_to_all(along_f, "slab", split_axis=4, concat_axis=1, tiled=True),
        depth_forward,
        precision=highest,
    )
    spectra = spectra * kinetic[None, :, :, None, :]
    along_a = jnp.einsum("bkftg,gtsa->bkfsa", spectra, depth_inverse, precision=highest)
    returned = lax.all_to_all(along_a, "slab", split_axis=4, concat_axis=2, tiled=True)
    rows_c = jnp.einsum("bkfsa,fsrc->bkarc", returned, second_inverse, precision=highest)
    lines_x = lax.all_to_all(rows_c, "pencil", split_axis=4, concat_axis=1, tiled=True)
    kinetic_part = jnp.einsum("bkarc,krx->bacx", lines_x, first_inverse, precision=highest)
    kinetic_part = kinetic_part / float(NG**3)
    applied = kinetic_part + potential[None] * orbitals
    filtered = jnp.where(
        unlocked[:, None, None, None] == 1,
        (applied - filter_center * orbitals) / filter_half,
        orbitals,
    )
    number = filtered.shape[0]
    flattened = filtered.reshape(number, -1)
    partial_intersection = jnp.dot(flattened, flattened.T, precision=highest) / float(NG**3)
    intersection = lax.psum(partial_intersection, ("slab", "pencil"))
    factor = jnp.linalg.cholesky(intersection)
    result = jax.scipy.linalg.solve_triangular(factor, flattened, lower=True)
    return result.reshape(filtered.shape)


def solution(mesh):
    slabs, pencils = mesh.shape["slab"], mesh.shape["pencil"]

    def local(orbitals, potential, unlocked):
        bands, rows_a, rows_c, length = orbitals.shape
        half = length // 4
        f_block = 2 * half // pencils
        chunks = half // (2 * slabs)
        fits = chunks > 0 and half % (2 * slabs) == 0 and rows_a % 8 == 0 and rows_c % 8 == 0 and f_block % 8 == 0
        if fits:
            return by_kernel(slabs, pencils, chunks, orbitals, potential, unlocked)
        return by_collectives(orbitals, potential, unlocked)

    in_specs = (P(None, "slab", "pencil", None), P("slab", "pencil", None), P())
    out_specs = P(None, "slab", "pencil", None)
    return jax.shard_map(local, mesh=mesh, in_specs=in_specs, out_specs=out_specs, check_vma=False)
```

```python
import functools
import math

import jax
import jax.numpy as jnp
import ml_dtypes
import numpy as np
from jax import lax
from jax.experimental import pallas as pl
from jax.experimental.pallas import tpu as pltpu
from jax.sharding import PartitionSpec as P

MESH = pl.DeviceIdType.MESH


def dft_tables(length, slabs, pencils, chunks):
    half = length // 4
    pair = half // (slabs * chunks)
    place = np.arange(length)
    modes = np.arange(2 * half) - half
    third = np.arange(half)

    def waves(mode):
        angle = 2.0 * np.pi / length * ((mode[:, None] * place[None, :]) % length)
        return np.cos(angle), np.sin(angle)

    cos_k, sin_k = waves(third)
    weight = np.where(third == 0, 1.0, 2.0)[:, None]

    def order(cosine, sine):
        both = np.stack([cosine, sine], 0).reshape(2, chunks, slabs, pair, length)
        return both.transpose(1, 2, 0, 3, 4).reshape(2 * half, length)

    forward_x = order(cos_k, -sin_k).T
    inverse_x = order(weight * cos_k, -weight * sin_k)
    cosine, sine = waves(modes)
    forward = np.stack([np.stack([cosine, sine], 1), np.stack([-sine, cosine], 1)], 0)
    inverse = np.stack([np.stack([cosine.T, -sine.T], 1), np.stack([sine.T, cosine.T], 1)], 0)
    f_block = 2 * half // pencils
    a_block = length // slabs
    c_block = length // pencils
    forward_a = forward.reshape(2, pencils, f_block, 2 * length).transpose(1, 0, 2, 3).reshape(4 * half, 2 * length)
    forward_c = forward.reshape(4 * half, 2 * length).T
    inverse_c = inverse.reshape(2, pencils, c_block, 4 * half).transpose(1, 0, 2, 3).reshape(2 * length, 4 * half).T
    inverse_a = inverse.reshape(2, slabs, a_block, 4 * half).transpose(1, 0, 2, 3).reshape(2 * length, 4 * half)
    tables = (forward_x, forward_a, forward_c, inverse_c, inverse_a, inverse_x)
    pairs = []
    for table in tables:
        high = table.astype(ml_dtypes.bfloat16)
        low = (table - high.astype(np.float64)).astype(ml_dtypes.bfloat16)
        pairs.append(np.stack([high, low], 0))
    return pairs


def split(value):
    high = value.astype(jnp.bfloat16)
    return high, (value - high.astype(jnp.float32)).astype(jnp.bfloat16)


def product(left, right):
    return jnp.dot(left, right, preferred_element_type=jnp.float32)


def from_left(table, value):
    high, low = split(value)
    return product(table[0], high) + (product(table[0], low) + product(table[1], high))


def from_right(value, table):
    high, low = split(value)
    return product(high, table[0]) + (product(low, table[0]) + product(high, table[1]))


def kernel(sizes, unlocked, orbitals, potential, fx, fa, fc, ic, ia, ix, row_k, row_f, col_s, out,
           lines, s1, r1, s2, r2, s3, r3, s4, r4, back, sums, g1, h1, g2, h2,
           own, send1, recv1, send2, recv2, send3, recv3, send4, recv4, gs1, gr1, gs2, gr2):
    slabs, pencils, chunks, pair, bands, length = sizes
    rows_a = orbitals.shape[1]
    rows_c = orbitals.shape[2]
    half = length // 4
    f_block = 2 * half // pencils
    wide = bands * rows_c
    i_s = lax.axis_index("slab")
    i_p = lax.axis_index("pencil")

    def slab_peer(d):
        return lax.rem(i_s + d, slabs)

    def pencil_peer(d):
        return lax.rem(i_p + d, pencils)

    barrier = pltpu.get_barrier_semaphore()
    for d in range(1, slabs):
        pl.semaphore_signal(barrier, inc=1, device_id=(slab_peer(d), i_p), device_id_type=MESH)
    for d in range(1, pencils):
        pl.semaphore_signal(barrier, inc=1, device_id=(i_s, pencil_peer(d)), device_id_type=MESH)

    def to_slab(d, src, dst, send, recv):
        return pltpu.make_async_remote_copy(
            src_ref=src, dst_ref=dst, send_sem=send, recv_sem=recv,
            device_id=(slab_peer(d), i_p), device_id_type=MESH)

    def to_pencil(d, src, dst, send, recv):
        return pltpu.make_async_remote_copy(
            src_ref=src, dst_ref=dst, send_sem=send, recv_sem=recv,
            device_id=(i_s, pencil_peer(d)), device_id_type=MESH)

    mine_a = pl.ds(pl.multiple_of(i_s * rows_a, 8), rows_a)
    mine_f = pl.ds(pl.multiple_of(i_p * f_block, 8), f_block)

    def copies(which, q):
        if which == 0:
            remote = [to_slab(d, s1.at[q, slab_peer(d)], r1.at[q, :, mine_a, :], send1.at[q, d], recv1.at[q, d])
                      for d in range(1, slabs)]
            local = pltpu.make_async_copy(s1.at[q, i_s], r1.at[q, :, mine_a, :], own.at[0, q])
        elif which == 1:
            remote = [to_pencil(d, s2.at[q, pencil_peer(d)], r2.at[q, i_p], send2.at[q, d], recv2.at[q, d])
                      for d in range(1, pencils)]
            local = pltpu.make_async_copy(s2.at[q, i_p], r2.at[q, i_p], own.at[1, q])
        elif which == 2:
            remote = [to_pencil(d, s3.at[q, pencil_peer(d)], r3.at[q, :, mine_f, :], send3.at[q, d], recv3.at[q, d])
                      for d in range(1, pencils)]
            local = pltpu.make_async_copy(s3.at[q, i_p], r3.at[q, :, mine_f, :], own.at[2, q])
        else:
            remote = [to_slab(d, s4.at[q, slab_peer(d)], r4.at[q, i_s], send4.at[q, d], recv4.at[q, d])
                      for d in range(1, slabs)]
            local = pltpu.make_async_copy(s4.at[q, i_s], r4.at[q, i_s], own.at[3, q])
        return remote, local

    def start(which, q):
        remote, local = copies(which, q)
        for copy in remote:
            copy.start()
        local.start()

    def arrived(which, q):
        remote, local = copies(which, q)
        for copy in remote:
            copy.wait_recv()
        local.wait()

    modes_x = 2 * half

    group = 4

    def forward_lines(g, carry):
        rows = jnp.concatenate(
            [orbitals[:, pl.ds(g * group + n, 1)].reshape(wide, length) for n in range(group)], 0)
        result = from_right(rows, fx)
        for n in range(group):
            turned = result[n * wide:(n + 1) * wide].T
            at = pl.multiple_of((g * group + n) * modes_x, modes_x)
            for t in range(lines.shape[0]):
                low, high = t * 128, min(t * 128 + 128, wide)
                lines[t, pl.ds(at, modes_x), 0:high - low] = turned[:, low:high]
        return carry

    lax.fori_loop(0, rows_a // group, forward_lines, 0)
    pl.semaphore_wait(barrier, slabs - 1 + pencils - 1)

    def line_rows(ref, i):
        parts = []
        for t in range(ref.shape[0]):
            size = min(128, wide - t * 128)
            parts.append(ref[t, pl.ds(i, rows_a, stride=modes_x), :][:, :size])
        return parts

    for q in range(chunks):
        for j in range(slabs):
            for r in range(2):
                parts = []
                for k in range(pair):
                    parts += line_rows(lines, ((q * slabs + j) * 2 + r) * pair + k)
                s1[q, j, r] = jnp.concatenate(parts, 1)
        start(0, q)

    packed = pair * wide

    def first_forward(q):
        arrived(0, q)
        result = from_left(fa, r1[q].reshape(2 * length, packed))
        s2[q] = result.reshape(pencils, 2, f_block, packed)
        start(1, q)

    def second(q):
        arrived(1, q)
        blocks = []
        for kb in range(pair * bands):
            lanes = slice(kb * rows_c, (kb + 1) * rows_c)
            blocks.append(jnp.concatenate([r2[q, p, r, :, lanes] for r in range(2) for p in range(pencils)], 1))
        spectrum = from_right(jnp.concatenate(blocks, 0), fc)
        mode_k = row_k[...] + (q * slabs * pair + i_s * pair).astype(jnp.float32)
        mode_f = row_f[...] + (i_p * f_block - half).astype(jnp.float32)
        squared = mode_k * mode_k + mode_f * mode_f + col_s[...]
        radius = float(half * half)
        kinetic = jnp.where(squared < radius, 4.0 * squared / radius, 0.0) * (1.0 / float(length**3))
        result = from_right(spectrum * kinetic, ic)
        for p in range(pencils):
            for r in range(2):
                lanes = slice((p * 2 + r) * rows_c, (p * 2 + r + 1) * rows_c)
                s3[q, p, r] = jnp.concatenate(
                    [result[kb * f_block:(kb + 1) * f_block, lanes] for kb in range(pair * bands)], 1)
        start(2, q)

    def first_inverse(q):
        arrived(2, q)
        result = from_left(ia, r3[q].reshape(4 * half, packed))
        s4[q] = result.reshape(slabs, 2, rows_a, packed)
        start(3, q)

    for step in range(chunks + 2):
        if step >= 2:
            first_inverse(step - 2)
        if step < chunks:
            first_forward(step)
        if 1 <= step <= chunks:
            second(step - 1)

    for q in range(chunks):
        arrived(3, q)
        for j in range(slabs):
            for r in range(2):
                value = r4[q, j, r]
                for k in range(pair):
                    i = ((q * slabs + j) * 2 + r) * pair + k
                    for t in range(back.shape[0]):
                        low, high = t * 128, min(t * 128 + 128, wide)
                        piece = value[:, k * wide + low:k * wide + high]
                        if high - low < 128:
                            piece = jnp.concatenate([piece, jnp.zeros((rows_a, 128 - high + low), jnp.float32)], 1)
                        back[t, pl.ds(i, rows_a, stride=modes_x), :] = piece

    sums[...] = jnp.zeros_like(sums)

    def inverse_lines(g, carry):
        spectra = []
        for n in range(group):
            at = pl.multiple_of((g * group + n) * modes_x, modes_x)
            spectra.append(jnp.concatenate(
                [back[t, pl.ds(at, modes_x), 0:min(128, wide - t * 128)] for t in range(back.shape[0])], 1).T)
        kinetic_parts = from_right(jnp.concatenate(spectra, 0), ix)
        for n in range(group):
            a = g * group + n
            kinetic_part = kinetic_parts[n * wide:(n + 1) * wide]
            level = potential[pl.ds(a, 1)].reshape(rows_c, length)
            filtered = []
            for b in range(bands):
                orbital = orbitals[b, pl.ds(a, 1)].reshape(rows_c, length)
                applied = kinetic_part[b * rows_c:(b + 1) * rows_c] + level * orbital
                value = jnp.where(unlocked[b] == 1, (applied - orbital) / 1.5, orbital)
                out[b, pl.ds(a, 1)] = value.reshape(1, rows_c, length)
                filtered.append(value)
            i = 0
            for b in range(bands):
                for e in range(b + 1):
                    squares = filtered[b] * filtered[e]
                    sums[i] += squares.reshape(rows_c // 8, 8, length).sum(0)
                    i += 1
        return carry

    lax.fori_loop(0, rows_a // group, inverse_lines, 0)

    total = jnp.sum(jnp.sum(sums[...], axis=1), axis=1, keepdims=True)
    g1[...] = jnp.broadcast_to(total, g1.shape)
    shares = [to_slab(d, g1, h1.at[i_s], gs1.at[d], gr1.at[d]) for d in range(1, slabs)]
    for copy in shares:
        copy.start()
    h1[pl.ds(i_s, 1)] = g1[...][None]
    for copy in shares:
        copy.wait()
    g2[...] = jnp.sum(h1[...], axis=0)
    shares = [to_pencil(d, g2, h2.at[i_p], gs2.at[d], gr2.at[d]) for d in range(1, pencils)]
    for copy in shares:
        copy.start()
    h2[pl.ds(i_p, 1)] = g2[...][None]
    for copy in shares:
        copy.wait()
    gram = jnp.sum(h2[...], axis=0) / float(length**3)

    factor = {}
    for b in range(bands):
        for e in range(b + 1):
            n = b * (b + 1) // 2 + e
            value = gram[n:n + 1, 0:1]
            for m in range(e):
                value = value - factor[b, m] * factor[e, m]
            factor[b, e] = jnp.sqrt(value) if b == e else value / factor[e, e]
    inverse = [1.0 / factor[b, b] for b in range(bands)]

    def solve_line(a, carry):
        solved = []
        for b in range(bands):
            value = out[b, pl.ds(a, 1)].reshape(rows_c, length)
            for m in range(b):
                value = value - factor[b, m] * solved[m]
            value = value * inverse[b]
            out[b, pl.ds(a, 1)] = value.reshape(1, rows_c, length)
            solved.append(value)
        return carry

    lax.fori_loop(0, rows_a, solve_line, 0)
    for which in range(4):
        for q in range(chunks):
            for copy in copies(which, q)[0]:
                copy.wait_send()


def by_kernel(slabs, pencils, chunks, orbitals, potential, unlocked):
    bands, rows_a, rows_c, length = orbitals.shape
    half = length // 4
    pair = half // (slabs * chunks)
    f_block = 2 * half // pencils
    wide = bands * rows_c
    packed = pair * wide
    tiles = -(-wide // 128)
    pairs = bands * (bands + 1) // 2
    tables = dft_tables(length, slabs, pencils, chunks)
    rows = np.arange(pair * bands * f_block)
    row_k = (rows // (bands * f_block)).astype(np.float32)[:, None]
    row_f = (rows % f_block).astype(np.float32)[:, None]
    col_s = ((np.arange(4 * half) % (2 * half) - half).astype(np.float32) ** 2)[None, :]
    vmem = pl.BlockSpec(memory_space=pltpu.VMEM)
    f32 = jnp.float32
    dma = pltpu.SemaphoreType.DMA
    scratch = [
        pltpu.VMEM((tiles, rows_a * 2 * half, 128), f32),
        pltpu.VMEM((chunks, slabs, 2, rows_a, packed), f32),
        pltpu.VMEM((chunks, 2, length, packed), f32),
        pltpu.VMEM((chunks, pencils, 2, f_block, packed), f32),
        pltpu.VMEM((chunks, pencils, 2, f_block, packed), f32),
        pltpu.VMEM((chunks, pencils, 2, f_block, packed), f32),
        pltpu.VMEM((chunks, 2, 2 * half, packed), f32),
        pltpu.VMEM((chunks, slabs, 2, rows_a, packed), f32),
        pltpu.VMEM((chunks, slabs, 2, rows_a, packed), f32),
        pltpu.VMEM((tiles, rows_a * 2 * half, 128), f32),
        pltpu.VMEM((pairs, 8, length), f32),
        pltpu.VMEM((pairs, 128), f32),
        pltpu.VMEM((slabs, pairs, 128), f32),
        pltpu.VMEM((pairs, 128), f32),
        pltpu.VMEM((pencils, pairs, 128), f32),
        dma((4, chunks)),
        dma((chunks, slabs)), dma((chunks, slabs)),
        dma((chunks, pencils)), dma((chunks, pencils)),
        dma((chunks, pencils)), dma((chunks, pencils)),
        dma((chunks, slabs)), dma((chunks, slabs)),
        dma((slabs,)), dma((slabs,)),
        dma((pencils,)), dma((pencils,)),
    ]
    flops = 2 * rows_a * wide * length * 2 * half * 6
    return pl.pallas_call(
        functools.partial(kernel, (slabs, pencils, chunks, pair, bands, length)),
        out_shape=jax.ShapeDtypeStruct(orbitals.shape, f32),
        in_specs=[pl.BlockSpec(memory_space=pltpu.SMEM)] + [vmem] * 11,
        out_specs=vmem,
        scratch_shapes=scratch,
        compiler_params=pltpu.CompilerParams(
            collective_id=0, has_side_effects=True, vmem_limit_bytes=56 * 1024 * 1024),
        cost_estimate=pl.CostEstimate(flops=flops, bytes_accessed=10 * 2**20, transcendentals=0),
    )(unlocked, orbitals, potential, *[jnp.asarray(t) for t in tables],
      jnp.asarray(row_k), jnp.asarray(row_f), jnp.asarray(col_s))


NG = 192


kinetic_scale = 4.0
filter_center = 1.0
filter_half = 1.5
highest = lax.Precision.HIGHEST


def frequencies(number, length):
    index = jnp.arange(number, dtype=jnp.int32)
    if number == length:
        return jnp.where(index < length // 2, index, index - length)
    return index - length // 4


def tables(number, length):
    modes = frequencies(number, length)
    places = jnp.arange(length, dtype=jnp.int32)
    product = places[:, None] * modes[None, :] % length
    angle = 2.0 * math.pi / length * product.astype(jnp.float32)
    return (jnp.cos(angle), jnp.sin(angle))


def forward_table(cosine, sine):
    return jnp.stack([jnp.stack([cosine, -sine], 1), jnp.stack([sine, cosine], 1)], 1)


def inverse_table(cosine, sine):
    cos_t = cosine.T
    sin_t = sine.T
    return jnp.stack([jnp.stack([cos_t, sin_t], 1), jnp.stack([-sin_t, cos_t], 1)], 1)


def by_collectives(orbitals, potential, unlocked):
    length = orbitals.shape[3]
    kept_modes = length // 2
    cos_k, sin_k = tables(kept_modes, length)
    cos_f, sin_f = tables(length, length)
    first_forward = jnp.stack([cos_k, -sin_k], 1)
    first_inverse = jnp.stack([cos_k.T, -sin_k.T], 1)
    second_forward = forward_table(cos_k, sin_k)
    second_inverse = inverse_table(cos_k, sin_k)
    depth_forward = forward_table(cos_f, sin_f)
    depth_inverse = inverse_table(cos_f, sin_f)
    pencil_block = kept_modes // lax.axis_size("pencil")
    slab_block = kept_modes // lax.axis_size("slab")
    kept_list = frequencies(kept_modes, length)
    third_modes = lax.dynamic_slice_in_dim(
        kept_list, lax.axis_index("pencil") * pencil_block, pencil_block
    ).astype(jnp.float32)
    second_modes = lax.dynamic_slice_in_dim(
        kept_list, lax.axis_index("slab") * slab_block, slab_block
    ).astype(jnp.float32)
    first_modes = frequencies(length, length).astype(jnp.float32)
    squared = (
        third_modes[:, None, None] ** 2
        + second_modes[None, :, None] ** 2
        + first_modes[None, None, :] ** 2
    )
    radius = float((length // 4) ** 2)
    kinetic = jnp.where(squared < radius, kinetic_scale * squared / radius, 0.0)
    lines_k = jnp.einsum("bacx,xrk->bacrk", orbitals, first_forward, precision=highest)
    along_f = jnp.einsum(
        "bacrk,crsf->baksf",
        lax.all_to_all(lines_k, "pencil", split_axis=4, concat_axis=2, tiled=True),
        second_forward,
        precision=highest,
    )
    spectra = jnp.einsum(
        "baksf,astg->bkftg",
        lax.all_to_all(along_f, "slab", split_axis=4, concat_axis=1, tiled=True),
        depth_forward,
        precision=highest,
    )
    spectra = spectra * kinetic[None, :, :, None, :]
    along_a = jnp.einsum("bkftg,gtsa->bkfsa", spectra, depth_inverse, precision=highest)
    returned = lax.all_to_all(along_a, "slab", split_axis=4, concat_axis=2, tiled=True)
    rows_c = jnp.einsum("bkfsa,fsrc->bkarc", returned, second_inverse, precision=highest)
    lines_x = lax.all_to_all(rows_c, "pencil", split_axis=4, concat_axis=1, tiled=True)
    kinetic_part = jnp.einsum("bkarc,krx->bacx", lines_x, first_inverse, precision=highest)
    kinetic_part = kinetic_part / float(NG**3)
    applied = kinetic_part + potential[None] * orbitals
    filtered = jnp.where(
        unlocked[:, None, None, None] == 1,
        (applied - filter_center * orbitals) / filter_half,
        orbitals,
    )
    number = filtered.shape[0]
    flattened = filtered.reshape(number, -1)
    partial_intersection = jnp.dot(flattened, flattened.T, precision=highest) / float(NG**3)
    intersection = lax.psum(partial_intersection, ("slab", "pencil"))
    factor = jnp.linalg.cholesky(intersection)
    result = jax.scipy.linalg.solve_triangular(factor, flattened, lower=True)
    return result.reshape(filtered.shape)


def solution(mesh):
    slabs, pencils = mesh.shape["slab"], mesh.shape["pencil"]

    def local(orbitals, potential, unlocked):
        bands, rows_a, rows_c, length = orbitals.shape
        half = length // 4
        f_block = 2 * half // pencils
        chunks = half // (2 * slabs)
        fits = chunks > 0 and half % (2 * slabs) == 0 and rows_a % 8 == 0 and rows_c % 8 == 0 and f_block % 8 == 0
        if fits:
            return by_kernel(slabs, pencils, chunks, orbitals, potential, unlocked)
        return by_collectives(orbitals, potential, unlocked)

    in_specs = (P(None, "slab", "pencil", None), P("slab", "pencil", None), P())
    out_specs = P(None, "slab", "pencil", None)
    return jax.shard_map(local, mesh=mesh, in_specs=in_specs, out_specs=out_specs, check_vma=False)
```

```python
import functools
import math

import jax
import jax.numpy as jnp
import ml_dtypes
import numpy as np
from jax import lax
from jax.experimental import pallas as pl
from jax.experimental.pallas import tpu as pltpu
from jax.sharding import PartitionSpec as P

MESH = pl.DeviceIdType.MESH


def dft_tables(length, slabs, pencils, chunks):
    half = length // 4
    pair = half // (slabs * chunks)
    place = np.arange(length)
    modes = np.arange(2 * half) - half
    third = np.arange(half)

    def waves(mode):
        angle = 2.0 * np.pi / length * ((mode[:, None] * place[None, :]) % length)
        return np.cos(angle), np.sin(angle)

    cos_k, sin_k = waves(third)
    weight = np.where(third == 0, 1.0, 2.0)[:, None]

    def order(cosine, sine):
        both = np.stack([cosine, sine], 0).reshape(2, chunks, slabs, pair, length)
        return both.transpose(1, 2, 0, 3, 4).reshape(2 * half, length)

    forward_x = order(cos_k, -sin_k).T
    inverse_x = order(weight * cos_k, -weight * sin_k)
    cosine, sine = waves(modes)
    forward = np.stack([np.stack([cosine, sine], 1), np.stack([-sine, cosine], 1)], 0)
    inverse = np.stack([np.stack([cosine.T, -sine.T], 1), np.stack([sine.T, cosine.T], 1)], 0)
    c_block = length // pencils
    forward_a = np.concatenate([cosine, sine], 0)
    forward_c = forward.reshape(4 * half, 2 * length).T
    inverse_c = inverse.reshape(2, pencils, c_block, 4 * half).transpose(1, 0, 2, 3).reshape(2 * length, 4 * half).T
    inverse_a = np.concatenate([cosine.T, sine.T], 0)
    tables = (forward_x, forward_a, forward_c, inverse_c, inverse_a, inverse_x)
    pairs = []
    for table in tables:
        high = table.astype(ml_dtypes.bfloat16)
        low = (table - high.astype(np.float64)).astype(ml_dtypes.bfloat16)
        pairs.append(np.stack([high, low], 0))
    return pairs


def split(value):
    high = value.astype(jnp.bfloat16)
    return high, (value - high.astype(jnp.float32)).astype(jnp.bfloat16)


def product(left, right):
    return jnp.dot(left, right, preferred_element_type=jnp.float32)


def from_left(table, value):
    high, low = split(value)
    return product(table[0], high) + (product(table[0], low) + product(table[1], high))


def from_right(value, table):
    high, low = split(value)
    return product(high, table[0]) + (product(low, table[0]) + product(high, table[1]))


def kernel(sizes, unlocked, orbitals, potential, fx, fa, fc, ic, ia, ix, row_k, row_f, col_s, out,
           lines, s1, r1, s2, r2, s3, r3, s4, r4, back, sums, g1, h1, g2, h2,
           own, send1, recv1, send2, recv2, send3, recv3, send4, recv4, gs1, gr1, gs2, gr2):
    slabs, pencils, chunks, pair, bands, length = sizes
    few = bands // 2
    rows_a = orbitals.shape[1]
    rows_c = orbitals.shape[2]
    half = length // 4
    f_block = 2 * half // pencils
    wide = few * rows_c
    packed = 2 * pair * wide
    i_s = lax.axis_index("slab")
    i_p = lax.axis_index("pencil")

    def slab_peer(d):
        return lax.rem(i_s + d, slabs)

    def pencil_peer(d):
        return lax.rem(i_p + d, pencils)

    barrier = pltpu.get_barrier_semaphore()
    for d in range(1, slabs):
        pl.semaphore_signal(barrier, inc=1, device_id=(slab_peer(d), i_p), device_id_type=MESH)
    for d in range(1, pencils):
        pl.semaphore_signal(barrier, inc=1, device_id=(i_s, pencil_peer(d)), device_id_type=MESH)

    def to_slab(d, src, dst, send, recv):
        return pltpu.make_async_remote_copy(
            src_ref=src, dst_ref=dst, send_sem=send, recv_sem=recv,
            device_id=(slab_peer(d), i_p), device_id_type=MESH)

    def to_pencil(d, src, dst, send, recv):
        return pltpu.make_async_remote_copy(
            src_ref=src, dst_ref=dst, send_sem=send, recv_sem=recv,
            device_id=(i_s, pencil_peer(d)), device_id_type=MESH)

    mine_a = pl.ds(pl.multiple_of(i_s * rows_a, 8), rows_a)
    mine_f = pl.ds(pl.multiple_of(i_p * f_block, 8), f_block)

    def copies(which, q):
        if which == 0:
            remote = [to_slab(d, s1.at[q, slab_peer(d)], r1.at[q, mine_a, :], send1.at[q, d], recv1.at[q, d])
                      for d in range(1, slabs)]
            local = pltpu.make_async_copy(s1.at[q, i_s], r1.at[q, mine_a, :], own.at[0, q])
        elif which == 1:
            remote = [to_pencil(d, s2.at[q, pencil_peer(d)], r2.at[q, i_p], send2.at[q, d], recv2.at[q, d])
                      for d in range(1, pencils)]
            local = pltpu.make_async_copy(s2.at[q, i_p], r2.at[q, i_p], own.at[1, q])
        elif which == 2:
            remote = [to_pencil(d, s3.at[q, pencil_peer(d)], r3.at[q, mine_f, :], send3.at[q, d], recv3.at[q, d])
                      for d in range(1, pencils)]
            local = pltpu.make_async_copy(s3.at[q, i_p], r3.at[q, mine_f, :], own.at[2, q])
        else:
            remote = [to_slab(d, s4.at[q, slab_peer(d)], r4.at[q, i_s], send4.at[q, d], recv4.at[q, d])
                      for d in range(1, slabs)]
            local = pltpu.make_async_copy(s4.at[q, i_s], r4.at[q, i_s], own.at[3, q])
        return remote, local

    def start(which, q):
        remote, local = copies(which, q)
        for copy in remote:
            copy.start()
        local.start()

    def arrived(which, q):
        remote, local = copies(which, q)
        for copy in remote:
            copy.wait_recv()
        local.wait()

    modes_x = 2 * half
    group = 8

    def forward_x(h):
        def body(g, carry):
            rows = jnp.concatenate(
                [orbitals[h * few:(h + 1) * few, pl.ds(g * group + n, 1)].reshape(wide, length)
                 for n in range(group)], 0)
            result = from_right(rows, fx)
            for n in range(group):
                at = pl.multiple_of((g * group + n) * modes_x, modes_x)
                lines[h, pl.ds(at, modes_x), 0:wide] = result[n * wide:(n + 1) * wide].T
            return carry

        lax.fori_loop(0, rows_a // group, body, 0)

    def send_lines(h):
        for q in range(chunks):
            for j in range(slabs):
                s1[h * chunks + q, j] = jnp.concatenate(
                    [lines[h, pl.ds(((q * slabs + j) * 2 + r) * pair + k, rows_a, stride=modes_x), :][:, :wide]
                     for r in range(2) for k in range(pair)], 1)
            start(0, h * chunks + q)

    middle = packed // 2

    def first_forward(q):
        arrived(0, q)
        result = from_left(fa, r1[q])
        cosine, sine = result[:2 * half], result[2 * half:]
        result = cosine + jnp.concatenate([sine[:, middle:], -sine[:, :middle]], 1)
        s2[q] = result.reshape(s2.shape[1:])
        start(1, q)

    def second(q):
        arrived(1, q)
        blocks = []
        for kb in range(pair * few):
            blocks.append(jnp.concatenate(
                [r2[q, p, :, r * middle + kb * rows_c:r * middle + (kb + 1) * rows_c]
                 for r in range(2) for p in range(pencils)], 1))
        spectrum = from_right(jnp.concatenate(blocks, 0), fc)
        mode_k = row_k[...] + (q % chunks * slabs * pair + i_s * pair).astype(jnp.float32)
        mode_f = row_f[...] + (i_p * f_block - half).astype(jnp.float32)
        squared = mode_k * mode_k + mode_f * mode_f + col_s[...]
        radius = float(half * half)
        kinetic = jnp.where(squared < radius, 4.0 * squared / radius, 0.0) * (1.0 / float(length**3))
        result = from_right(spectrum * kinetic, ic)
        for p in range(pencils):
            s3[q, p] = jnp.concatenate(
                [result[kb * f_block:(kb + 1) * f_block, (p * 2 + r) * rows_c:(p * 2 + r + 1) * rows_c]
                 for r in range(2) for kb in range(pair * few)], 1)
        start(2, q)

    def first_inverse(q):
        arrived(2, q)
        result = from_left(ia, r3[q])
        cosine, sine = result[:length], result[length:]
        result = cosine + jnp.concatenate([-sine[:, middle:], sine[:, :middle]], 1)
        s4[q] = result.reshape(s4.shape[1:])
        start(3, q)

    def take_lines(h, q):
        arrived(3, h * chunks + q)
        unused = jnp.zeros((rows_a, 128 - wide), jnp.float32)
        for j in range(slabs):
            value = r4[h * chunks + q, j]
            for r in range(2):
                for k in range(pair):
                    piece = value[:, r * middle + k * wide:r * middle + (k + 1) * wide]
                    back[h, pl.ds(((q * slabs + j) * 2 + r) * pair + k, rows_a, stride=modes_x), :] = (
                        jnp.concatenate([piece, unused], 1))

    def inverse_x(h):
        def body(g, carry):
            spectra = []
            for n in range(group):
                at = pl.multiple_of((g * group + n) * modes_x, modes_x)
                spectra.append(back[h, pl.ds(at, modes_x), 0:wide].T)
            kinetic_parts = from_right(jnp.concatenate(spectra, 0), ix)
            for n in range(group):
                a = g * group + n
                level = potential[pl.ds(a, 1)].reshape(rows_c, length)
                filtered = [out[b, pl.ds(a, 1)].reshape(rows_c, length) for b in range(h * few)]
                for b in range(few):
                    orbital = orbitals[h * few + b, pl.ds(a, 1)].reshape(rows_c, length)
                    kinetic_part = kinetic_parts[n * wide + b * rows_c:n * wide + (b + 1) * rows_c]
                    applied = kinetic_part + level * orbital
                    value = jnp.where(unlocked[h * few + b] == 1, (applied - orbital) / 1.5, orbital)
                    out[h * few + b, pl.ds(a, 1)] = value.reshape(1, rows_c, length)
                    filtered.append(value)
                for b in range(h * few, (h + 1) * few):
                    for e in range(b + 1):
                        squares = filtered[b] * filtered[e]
                        sums[b * (b + 1) // 2 + e] += squares.reshape(rows_c // 8, 8, length).sum(0)
            return carry

        lax.fori_loop(0, rows_a // group, body, 0)

    sums[...] = jnp.zeros_like(sums)
    forward_x(0)
    pl.semaphore_wait(barrier, slabs - 1 + pencils - 1)
    send_lines(0)
    forward_x(1)
    send_lines(1)
    last = 2 * chunks
    for step in range(last + 1):
        if step >= 2:
            first_inverse(step - 2)
        if step < last:
            first_forward(step)
        if step >= 1:
            second(step - 1)
    for q in range(chunks):
        take_lines(0, q)
    first_inverse(last - 1)
    inverse_x(0)
    for q in range(chunks):
        take_lines(1, q)
    inverse_x(1)

    total = jnp.sum(jnp.sum(sums[...], axis=1), axis=1, keepdims=True)
    g1[...] = jnp.broadcast_to(total, g1.shape)
    shares = [to_slab(d, g1, h1.at[i_s], gs1.at[d], gr1.at[d]) for d in range(1, slabs)]
    for copy in shares:
        copy.start()
    h1[pl.ds(i_s, 1)] = g1[...][None]
    for copy in shares:
        copy.wait()
    g2[...] = jnp.sum(h1[...], axis=0)
    shares = [to_pencil(d, g2, h2.at[i_p], gs2.at[d], gr2.at[d]) for d in range(1, pencils)]
    for copy in shares:
        copy.start()
    h2[pl.ds(i_p, 1)] = g2[...][None]
    for copy in shares:
        copy.wait()
    gram = jnp.sum(h2[...], axis=0) / float(length**3)

    factor = {}
    for b in range(bands):
        for e in range(b + 1):
            n = b * (b + 1) // 2 + e
            value = gram[n:n + 1, 0:1]
            for m in range(e):
                value = value - factor[b, m] * factor[e, m]
            factor[b, e] = jnp.sqrt(value) if b == e else value / factor[e, e]
    inverse = [1.0 / factor[b, b] for b in range(bands)]

    def solve_line(a, carry):
        solved = []
        for b in range(bands):
            value = out[b, pl.ds(a, 1)].reshape(rows_c, length)
            for m in range(b):
                value = value - factor[b, m] * solved[m]
            value = value * inverse[b]
            out[b, pl.ds(a, 1)] = value.reshape(1, rows_c, length)
            solved.append(value)
        return carry

    lax.fori_loop(0, rows_a, solve_line, 0)
    for which in range(4):
        for q in range(2 * chunks):
            for copy in copies(which, q)[0]:
                copy.wait_send()


def by_kernel(slabs, pencils, chunks, orbitals, potential, unlocked):
    bands, rows_a, rows_c, length = orbitals.shape
    half = length // 4
    pair = half // (slabs * chunks)
    f_block = 2 * half // pencils
    few = bands // 2
    parts = 2 * chunks
    packed = 2 * pair * few * rows_c
    pairs = bands * (bands + 1) // 2
    tables = dft_tables(length, slabs, pencils, chunks)
    rows = np.arange(pair * few * f_block)
    row_k = (rows // (few * f_block)).astype(np.float32)[:, None]
    row_f = (rows % f_block).astype(np.float32)[:, None]
    col_s = ((np.arange(4 * half) % (2 * half) - half).astype(np.float32) ** 2)[None, :]
    vmem = pl.BlockSpec(memory_space=pltpu.VMEM)
    f32 = jnp.float32
    dma = pltpu.SemaphoreType.DMA
    scratch = [
        pltpu.VMEM((2, rows_a * 2 * half, 128), f32),
        pltpu.VMEM((parts, slabs, rows_a, packed), f32),
        pltpu.VMEM((parts, length, packed), f32),
        pltpu.VMEM((parts, pencils, f_block, packed), f32),
        pltpu.VMEM((parts, pencils, f_block, packed), f32),
        pltpu.VMEM((parts, pencils, f_block, packed), f32),
        pltpu.VMEM((parts, 2 * half, packed), f32),
        pltpu.VMEM((parts, slabs, rows_a, packed), f32),
        pltpu.VMEM((parts, slabs, rows_a, packed), f32),
        pltpu.VMEM((2, rows_a * 2 * half, 128), f32),
        pltpu.VMEM((pairs, 8, length), f32),
        pltpu.VMEM((pairs, 128), f32),
        pltpu.VMEM((slabs, pairs, 128), f32),
        pltpu.VMEM((pairs, 128), f32),
        pltpu.VMEM((pencils, pairs, 128), f32),
        dma((4, parts)),
        dma((parts, slabs)), dma((parts, slabs)),
        dma((parts, pencils)), dma((parts, pencils)),
        dma((parts, pencils)), dma((parts, pencils)),
        dma((parts, slabs)), dma((parts, slabs)),
        dma((slabs,)), dma((slabs,)),
        dma((pencils,)), dma((pencils,)),
    ]
    flops = 2 * rows_a * bands * rows_c * length * 2 * half * 6
    return pl.pallas_call(
        functools.partial(kernel, (slabs, pencils, chunks, pair, bands, length)),
        out_shape=jax.ShapeDtypeStruct(orbitals.shape, f32),
        in_specs=[pl.BlockSpec(memory_space=pltpu.SMEM)] + [vmem] * 11,
        out_specs=vmem,
        scratch_shapes=scratch,
        compiler_params=pltpu.CompilerParams(
            collective_id=0, has_side_effects=True, vmem_limit_bytes=56 * 1024 * 1024),
        cost_estimate=pl.CostEstimate(flops=flops, bytes_accessed=10 * 2**20, transcendentals=0),
    )(unlocked, orbitals, potential, *[jnp.asarray(t) for t in tables],
      jnp.asarray(row_k), jnp.asarray(row_f), jnp.asarray(col_s))


NG = 192


kinetic_scale = 4.0
filter_center = 1.0
filter_half = 1.5
highest = lax.Precision.HIGHEST


def frequencies(number, length):
    index = jnp.arange(number, dtype=jnp.int32)
    if number == length:
        return jnp.where(index < length // 2, index, index - length)
    return index - length // 4


def tables(number, length):
    modes = frequencies(number, length)
    places = jnp.arange(length, dtype=jnp.int32)
    product = places[:, None] * modes[None, :] % length
    angle = 2.0 * math.pi / length * product.astype(jnp.float32)
    return (jnp.cos(angle), jnp.sin(angle))


def forward_table(cosine, sine):
    return jnp.stack([jnp.stack([cosine, -sine], 1), jnp.stack([sine, cosine], 1)], 1)


def inverse_table(cosine, sine):
    cos_t = cosine.T
    sin_t = sine.T
    return jnp.stack([jnp.stack([cos_t, sin_t], 1), jnp.stack([-sin_t, cos_t], 1)], 1)


def by_collectives(orbitals, potential, unlocked):
    length = orbitals.shape[3]
    kept_modes = length // 2
    cos_k, sin_k = tables(kept_modes, length)
    cos_f, sin_f = tables(length, length)
    first_forward = jnp.stack([cos_k, -sin_k], 1)
    first_inverse = jnp.stack([cos_k.T, -sin_k.T], 1)
    second_forward = forward_table(cos_k, sin_k)
    second_inverse = inverse_table(cos_k, sin_k)
    depth_forward = forward_table(cos_f, sin_f)
    depth_inverse = inverse_table(cos_f, sin_f)
    pencil_block = kept_modes // lax.axis_size("pencil")
    slab_block = kept_modes // lax.axis_size("slab")
    kept_list = frequencies(kept_modes, length)
    third_modes = lax.dynamic_slice_in_dim(
        kept_list, lax.axis_index("pencil") * pencil_block, pencil_block
    ).astype(jnp.float32)
    second_modes = lax.dynamic_slice_in_dim(
        kept_list, lax.axis_index("slab") * slab_block, slab_block
    ).astype(jnp.float32)
    first_modes = frequencies(length, length).astype(jnp.float32)
    squared = (
        third_modes[:, None, None] ** 2
        + second_modes[None, :, None] ** 2
        + first_modes[None, None, :] ** 2
    )
    radius = float((length // 4) ** 2)
    kinetic = jnp.where(squared < radius, kinetic_scale * squared / radius, 0.0)
    lines_k = jnp.einsum("bacx,xrk->bacrk", orbitals, first_forward, precision=highest)
    along_f = jnp.einsum(
        "bacrk,crsf->baksf",
        lax.all_to_all(lines_k, "pencil", split_axis=4, concat_axis=2, tiled=True),
        second_forward,
        precision=highest,
    )
    spectra = jnp.einsum(
        "baksf,astg->bkftg",
        lax.all_to_all(along_f, "slab", split_axis=4, concat_axis=1, tiled=True),
        depth_forward,
        precision=highest,
    )
    spectra = spectra * kinetic[None, :, :, None, :]
    along_a = jnp.einsum("bkftg,gtsa->bkfsa", spectra, depth_inverse, precision=highest)
    returned = lax.all_to_all(along_a, "slab", split_axis=4, concat_axis=2, tiled=True)
    rows_c = jnp.einsum("bkfsa,fsrc->bkarc", returned, second_inverse, precision=highest)
    lines_x = lax.all_to_all(rows_c, "pencil", split_axis=4, concat_axis=1, tiled=True)
    kinetic_part = jnp.einsum("bkarc,krx->bacx", lines_x, first_inverse, precision=highest)
    kinetic_part = kinetic_part / float(NG**3)
    applied = kinetic_part + potential[None] * orbitals
    filtered = jnp.where(
        unlocked[:, None, None, None] == 1,
        (applied - filter_center * orbitals) / filter_half,
        orbitals,
    )
    number = filtered.shape[0]
    flattened = filtered.reshape(number, -1)
    partial_intersection = jnp.dot(flattened, flattened.T, precision=highest) / float(NG**3)
    intersection = lax.psum(partial_intersection, ("slab", "pencil"))
    factor = jnp.linalg.cholesky(intersection)
    result = jax.scipy.linalg.solve_triangular(factor, flattened, lower=True)
    return result.reshape(filtered.shape)


def solution(mesh):
    slabs, pencils = mesh.shape["slab"], mesh.shape["pencil"]

    def local(orbitals, potential, unlocked):
        bands, rows_a, rows_c, length = orbitals.shape
        half = length // 4
        f_block = 2 * half // pencils
        chunks = half // (2 * slabs)
        even = bands % 2 == 0 and bands // 2 * rows_c <= 128 and chunks > 0 and half % (2 * slabs) == 0
        fits = even and rows_a % 8 == 0 and rows_c % 8 == 0 and f_block % 8 == 0
        if fits:
            return by_kernel(slabs, pencils, chunks, orbitals, potential, unlocked)
        return by_collectives(orbitals, potential, unlocked)

    in_specs = (P(None, "slab", "pencil", None), P("slab", "pencil", None), P())
    out_specs = P(None, "slab", "pencil", None)
    return jax.shard_map(local, mesh=mesh, in_specs=in_specs, out_specs=out_specs, check_vma=False)
```

```python
import functools
import math

import jax
import jax.numpy as jnp
import ml_dtypes
import numpy as np
from jax import lax
from jax.experimental import pallas as pl
from jax.experimental.pallas import tpu as pltpu
from jax.sharding import PartitionSpec as P

MESH = pl.DeviceIdType.MESH


def dft_tables(length, slabs, pencils, chunks):
    half = length // 4
    pair = half // (slabs * chunks)
    place = np.arange(length)
    modes = np.arange(2 * half) - half
    third = np.arange(half)

    def waves(mode):
        angle = 2.0 * np.pi / length * ((mode[:, None] * place[None, :]) % length)
        return np.cos(angle), np.sin(angle)

    cos_k, sin_k = waves(third)
    weight = np.where(third == 0, 1.0, 2.0)[:, None]

    def order(cosine, sine):
        both = np.stack([cosine, sine], 0).reshape(2, chunks, slabs, pair, length)
        return both.transpose(1, 2, 0, 3, 4).reshape(2 * half, length)

    forward_x = order(cos_k, -sin_k).T
    inverse_x = order(weight * cos_k, -weight * sin_k)
    cosine, sine = waves(modes)
    forward = np.stack([np.stack([cosine, sine], 1), np.stack([-sine, cosine], 1)], 0)
    inverse = np.stack([np.stack([cosine.T, -sine.T], 1), np.stack([sine.T, cosine.T], 1)], 0)
    c_block = length // pencils
    forward_a = np.concatenate([cosine, sine], 0)
    forward_c = forward.reshape(4 * half, 2 * length).T
    inverse_c = inverse.reshape(2, pencils, c_block, 4 * half).transpose(1, 0, 2, 3).reshape(2 * length, 4 * half).T
    inverse_a = np.concatenate([cosine.T, sine.T], 0)
    tables = (forward_x, forward_a, forward_c, inverse_c, inverse_a, inverse_x)
    pairs = []
    for table in tables:
        high = table.astype(ml_dtypes.bfloat16)
        low = (table - high.astype(np.float64)).astype(ml_dtypes.bfloat16)
        pairs.append(np.stack([high, low], 0))
    return pairs


def split(value):
    high = value.astype(jnp.bfloat16)
    return high, (value - high.astype(jnp.float32)).astype(jnp.bfloat16)


def product(left, right):
    return jnp.dot(left, right, preferred_element_type=jnp.float32)


def from_left(table, value):
    high, low = split(value)
    return product(table[0], high) + (product(table[0], low) + product(table[1], high))


def from_right(value, table):
    high, low = split(value)
    return product(high, table[0]) + (product(low, table[0]) + product(high, table[1]))


def kernel(sizes, unlocked, orbitals, potential, fx, fa, fc, ic, ia, ix, row_k, row_f, col_s, out,
           lines, s1, r1, s2, r2, s3, r3, s4, r4, back, sums, g1, h1, g2, h2,
           own, send1, recv1, send2, recv2, send3, recv3, send4, recv4, gs1, gr1, gs2, gr2):
    slabs, pencils, chunks, pair, bands, length = sizes
    few = bands // 2
    rows_a = orbitals.shape[1]
    rows_c = orbitals.shape[2]
    half = length // 4
    f_block = 2 * half // pencils
    wide = few * rows_c
    packed = 2 * pair * wide
    i_s = lax.axis_index("slab")
    i_p = lax.axis_index("pencil")

    def slab_peer(d):
        return lax.rem(i_s + d, slabs)

    def pencil_peer(d):
        return lax.rem(i_p + d, pencils)

    barrier = pltpu.get_barrier_semaphore()
    for d in range(1, slabs):
        pl.semaphore_signal(barrier, inc=1, device_id=(slab_peer(d), i_p), device_id_type=MESH)
    for d in range(1, pencils):
        pl.semaphore_signal(barrier, inc=1, device_id=(i_s, pencil_peer(d)), device_id_type=MESH)

    def to_slab(d, src, dst, send, recv):
        return pltpu.make_async_remote_copy(
            src_ref=src, dst_ref=dst, send_sem=send, recv_sem=recv,
            device_id=(slab_peer(d), i_p), device_id_type=MESH)

    def to_pencil(d, src, dst, send, recv):
        return pltpu.make_async_remote_copy(
            src_ref=src, dst_ref=dst, send_sem=send, recv_sem=recv,
            device_id=(i_s, pencil_peer(d)), device_id_type=MESH)

    mine_a = pl.ds(pl.multiple_of(i_s * rows_a, 8), rows_a)
    mine_f = pl.ds(pl.multiple_of(i_p * f_block, 8), f_block)

    def copies(which, q):
        if which == 0:
            remote = [to_slab(d, s1.at[q, slab_peer(d)], r1.at[q, mine_a, :], send1.at[q, d], recv1.at[q, d])
                      for d in range(1, slabs)]
            local = pltpu.make_async_copy(s1.at[q, i_s], r1.at[q, mine_a, :], own.at[0, q])
        elif which == 1:
            remote = [to_pencil(d, s2.at[q, pencil_peer(d)], r2.at[q, i_p], send2.at[q, d], recv2.at[q, d])
                      for d in range(1, pencils)]
            local = pltpu.make_async_copy(s2.at[q, i_p], r2.at[q, i_p], own.at[1, q])
        elif which == 2:
            remote = [to_pencil(d, s3.at[q, pencil_peer(d)], r3.at[q, mine_f, :], send3.at[q, d], recv3.at[q, d])
                      for d in range(1, pencils)]
            local = pltpu.make_async_copy(s3.at[q, i_p], r3.at[q, mine_f, :], own.at[2, q])
        else:
            remote = [to_slab(d, s4.at[q, slab_peer(d)], r4.at[q, i_s], send4.at[q, d], recv4.at[q, d])
                      for d in range(1, slabs)]
            local = pltpu.make_async_copy(s4.at[q, i_s], r4.at[q, i_s], own.at[3, q])
        return remote, local

    def start(which, q):
        remote, local = copies(which, q)
        for copy in remote:
            copy.start()
        local.start()

    def arrived(which, q):
        remote, local = copies(which, q)
        for copy in remote:
            copy.wait_recv()
        local.wait()

    modes_x = 2 * half
    group = 8

    def forward_x(h):
        def body(g, carry):
            rows = jnp.concatenate(
                [orbitals[h * few:(h + 1) * few, pl.ds(g * group + n, 1)].reshape(wide, length)
                 for n in range(group)], 0)
            result = from_right(rows, fx)
            for n in range(group):
                at = pl.multiple_of((g * group + n) * modes_x, modes_x)
                lines[h, pl.ds(at, modes_x), 0:wide] = result[n * wide:(n + 1) * wide].T
            return carry

        lax.fori_loop(0, rows_a // group, body, 0)

    def send_lines(h):
        for q in range(chunks):
            for j in range(slabs):
                s1[h * chunks + q, j] = jnp.concatenate(
                    [lines[h, pl.ds(((q * slabs + j) * 2 + r) * pair + k, rows_a, stride=modes_x), :][:, :wide]
                     for r in range(2) for k in range(pair)], 1)
            if h == 0:
                start(0, q)

    middle = packed // 2

    def first_forward(q):
        arrived(0, q)
        if q + chunks < 2 * chunks:
            start(0, q + chunks)
        result = from_left(fa, r1[q])
        cosine, sine = result[:2 * half], result[2 * half:]
        result = cosine + jnp.concatenate([sine[:, middle:], -sine[:, :middle]], 1)
        s2[q] = result.reshape(s2.shape[1:])
        start(1, q)

    def second(q):
        arrived(1, q)
        blocks = []
        for kb in range(pair * few):
            blocks.append(jnp.concatenate(
                [r2[q, p, :, r * middle + kb * rows_c:r * middle + (kb + 1) * rows_c]
                 for r in range(2) for p in range(pencils)], 1))
        spectrum = from_right(jnp.concatenate(blocks, 0), fc)
        mode_k = row_k[...] + (q % chunks * slabs * pair + i_s * pair).astype(jnp.float32)
        mode_f = row_f[...] + (i_p * f_block - half).astype(jnp.float32)
        squared = mode_k * mode_k + mode_f * mode_f + col_s[...]
        radius = float(half * half)
        kinetic = jnp.where(squared < radius, 4.0 * squared / radius, 0.0) * (1.0 / float(length**3))
        result = from_right(spectrum * kinetic, ic)
        for p in range(pencils):
            s3[q, p] = jnp.concatenate(
                [result[kb * f_block:(kb + 1) * f_block, (p * 2 + r) * rows_c:(p * 2 + r + 1) * rows_c]
                 for r in range(2) for kb in range(pair * few)], 1)
        start(2, q)

    def first_inverse(q):
        arrived(2, q)
        result = from_left(ia, r3[q])
        cosine, sine = result[:length], result[length:]
        result = cosine + jnp.concatenate([-sine[:, middle:], sine[:, :middle]], 1)
        s4[q] = result.reshape(s4.shape[1:])
        start(3, q)

    def take_lines(h, q):
        arrived(3, h * chunks + q)
        unused = jnp.zeros((rows_a, 128 - wide), jnp.float32)
        for j in range(slabs):
            value = r4[h * chunks + q, j]
            for r in range(2):
                for k in range(pair):
                    piece = value[:, r * middle + k * wide:r * middle + (k + 1) * wide]
                    back[h, pl.ds(((q * slabs + j) * 2 + r) * pair + k, rows_a, stride=modes_x), :] = (
                        jnp.concatenate([piece, unused], 1))

    def inverse_x(h):
        def body(g, carry):
            spectra = []
            for n in range(group):
                at = pl.multiple_of((g * group + n) * modes_x, modes_x)
                spectra.append(back[h, pl.ds(at, modes_x), 0:wide].T)
            kinetic_parts = from_right(jnp.concatenate(spectra, 0), ix)
            for n in range(group):
                a = g * group + n
                level = potential[pl.ds(a, 1)].reshape(rows_c, length)
                filtered = [out[b, pl.ds(a, 1)].reshape(rows_c, length) for b in range(h * few)]
                for b in range(few):
                    orbital = orbitals[h * few + b, pl.ds(a, 1)].reshape(rows_c, length)
                    kinetic_part = kinetic_parts[n * wide + b * rows_c:n * wide + (b + 1) * rows_c]
                    applied = kinetic_part + level * orbital
                    value = jnp.where(unlocked[h * few + b] == 1, (applied - orbital) / 1.5, orbital)
                    out[h * few + b, pl.ds(a, 1)] = value.reshape(1, rows_c, length)
                    filtered.append(value)
                for b in range(h * few, (h + 1) * few):
                    for e in range(b + 1):
                        squares = filtered[b] * filtered[e]
                        sums[b * (b + 1) // 2 + e] += squares.reshape(rows_c // 8, 8, length).sum(0)
            return carry

        lax.fori_loop(0, rows_a // group, body, 0)

    sums[...] = jnp.zeros_like(sums)
    forward_x(0)
    pl.semaphore_wait(barrier, slabs - 1 + pencils - 1)
    send_lines(0)
    forward_x(1)
    send_lines(1)
    last = 2 * chunks
    for step in range(last + 1):
        if step < last:
            first_forward(step)
        if step >= 1:
            second(step - 1)
        if step >= 2:
            first_inverse(step - 2)
    for q in range(chunks):
        take_lines(0, q)
    first_inverse(last - 1)
    inverse_x(0)
    for q in range(chunks):
        take_lines(1, q)
    inverse_x(1)

    total = jnp.sum(jnp.sum(sums[...], axis=1), axis=1, keepdims=True)
    g1[...] = jnp.broadcast_to(total, g1.shape)
    shares = [to_slab(d, g1, h1.at[i_s], gs1.at[d], gr1.at[d]) for d in range(1, slabs)]
    for copy in shares:
        copy.start()
    h1[pl.ds(i_s, 1)] = g1[...][None]
    for copy in shares:
        copy.wait()
    g2[...] = jnp.sum(h1[...], axis=0)
    shares = [to_pencil(d, g2, h2.at[i_p], gs2.at[d], gr2.at[d]) for d in range(1, pencils)]
    for copy in shares:
        copy.start()
    h2[pl.ds(i_p, 1)] = g2[...][None]
    for copy in shares:
        copy.wait()
    gram = jnp.sum(h2[...], axis=0) / float(length**3)

    factor = {}
    for b in range(bands):
        for e in range(b + 1):
            n = b * (b + 1) // 2 + e
            value = gram[n:n + 1, 0:1]
            for m in range(e):
                value = value - factor[b, m] * factor[e, m]
            factor[b, e] = jnp.sqrt(value) if b == e else value / factor[e, e]
    inverse = [1.0 / factor[b, b] for b in range(bands)]

    def solve_line(a, carry):
        solved = []
        for b in range(bands):
            value = out[b, pl.ds(a, 1)].reshape(rows_c, length)
            for m in range(b):
                value = value - factor[b, m] * solved[m]
            value = value * inverse[b]
            out[b, pl.ds(a, 1)] = value.reshape(1, rows_c, length)
            solved.append(value)
        return carry

    lax.fori_loop(0, rows_a, solve_line, 0)
    for which in range(4):
        for q in range(2 * chunks):
            for copy in copies(which, q)[0]:
                copy.wait_send()


def by_kernel(slabs, pencils, chunks, orbitals, potential, unlocked):
    bands, rows_a, rows_c, length = orbitals.shape
    half = length // 4
    pair = half // (slabs * chunks)
    f_block = 2 * half // pencils
    few = bands // 2
    parts = 2 * chunks
    packed = 2 * pair * few * rows_c
    pairs = bands * (bands + 1) // 2
    tables = dft_tables(length, slabs, pencils, chunks)
    rows = np.arange(pair * few * f_block)
    row_k = (rows // (few * f_block)).astype(np.float32)[:, None]
    row_f = (rows % f_block).astype(np.float32)[:, None]
    col_s = ((np.arange(4 * half) % (2 * half) - half).astype(np.float32) ** 2)[None, :]
    vmem = pl.BlockSpec(memory_space=pltpu.VMEM)
    f32 = jnp.float32
    dma = pltpu.SemaphoreType.DMA
    scratch = [
        pltpu.VMEM((2, rows_a * 2 * half, 128), f32),
        pltpu.VMEM((parts, slabs, rows_a, packed), f32),
        pltpu.VMEM((parts, length, packed), f32),
        pltpu.VMEM((parts, pencils, f_block, packed), f32),
        pltpu.VMEM((parts, pencils, f_block, packed), f32),
        pltpu.VMEM((parts, pencils, f_block, packed), f32),
        pltpu.VMEM((parts, 2 * half, packed), f32),
        pltpu.VMEM((parts, slabs, rows_a, packed), f32),
        pltpu.VMEM((parts, slabs, rows_a, packed), f32),
        pltpu.VMEM((2, rows_a * 2 * half, 128), f32),
        pltpu.VMEM((pairs, 8, length), f32),
        pltpu.VMEM((pairs, 128), f32),
        pltpu.VMEM((slabs, pairs, 128), f32),
        pltpu.VMEM((pairs, 128), f32),
        pltpu.VMEM((pencils, pairs, 128), f32),
        dma((4, parts)),
        dma((parts, slabs)), dma((parts, slabs)),
        dma((parts, pencils)), dma((parts, pencils)),
        dma((parts, pencils)), dma((parts, pencils)),
        dma((parts, slabs)), dma((parts, slabs)),
        dma((slabs,)), dma((slabs,)),
        dma((pencils,)), dma((pencils,)),
    ]
    flops = 2 * rows_a * bands * rows_c * length * 2 * half * 6
    return pl.pallas_call(
        functools.partial(kernel, (slabs, pencils, chunks, pair, bands, length)),
        out_shape=jax.ShapeDtypeStruct(orbitals.shape, f32),
        in_specs=[pl.BlockSpec(memory_space=pltpu.SMEM)] + [vmem] * 11,
        out_specs=vmem,
        scratch_shapes=scratch,
        compiler_params=pltpu.CompilerParams(
            collective_id=0, has_side_effects=True, vmem_limit_bytes=56 * 1024 * 1024),
        cost_estimate=pl.CostEstimate(flops=flops, bytes_accessed=10 * 2**20, transcendentals=0),
    )(unlocked, orbitals, potential, *[jnp.asarray(t) for t in tables],
      jnp.asarray(row_k), jnp.asarray(row_f), jnp.asarray(col_s))


NG = 192


kinetic_scale = 4.0
filter_center = 1.0
filter_half = 1.5
highest = lax.Precision.HIGHEST


def frequencies(number, length):
    index = jnp.arange(number, dtype=jnp.int32)
    if number == length:
        return jnp.where(index < length // 2, index, index - length)
    return index - length // 4


def tables(number, length):
    modes = frequencies(number, length)
    places = jnp.arange(length, dtype=jnp.int32)
    product = places[:, None] * modes[None, :] % length
    angle = 2.0 * math.pi / length * product.astype(jnp.float32)
    return (jnp.cos(angle), jnp.sin(angle))


def forward_table(cosine, sine):
    return jnp.stack([jnp.stack([cosine, -sine], 1), jnp.stack([sine, cosine], 1)], 1)


def inverse_table(cosine, sine):
    cos_t = cosine.T
    sin_t = sine.T
    return jnp.stack([jnp.stack([cos_t, sin_t], 1), jnp.stack([-sin_t, cos_t], 1)], 1)


def by_collectives(orbitals, potential, unlocked):
    length = orbitals.shape[3]
    kept_modes = length // 2
    cos_k, sin_k = tables(kept_modes, length)
    cos_f, sin_f = tables(length, length)
    first_forward = jnp.stack([cos_k, -sin_k], 1)
    first_inverse = jnp.stack([cos_k.T, -sin_k.T], 1)
    second_forward = forward_table(cos_k, sin_k)
    second_inverse = inverse_table(cos_k, sin_k)
    depth_forward = forward_table(cos_f, sin_f)
    depth_inverse = inverse_table(cos_f, sin_f)
    pencil_block = kept_modes // lax.axis_size("pencil")
    slab_block = kept_modes // lax.axis_size("slab")
    kept_list = frequencies(kept_modes, length)
    third_modes = lax.dynamic_slice_in_dim(
        kept_list, lax.axis_index("pencil") * pencil_block, pencil_block
    ).astype(jnp.float32)
    second_modes = lax.dynamic_slice_in_dim(
        kept_list, lax.axis_index("slab") * slab_block, slab_block
    ).astype(jnp.float32)
    first_modes = frequencies(length, length).astype(jnp.float32)
    squared = (
        third_modes[:, None, None] ** 2
        + second_modes[None, :, None] ** 2
        + first_modes[None, None, :] ** 2
    )
    radius = float((length // 4) ** 2)
    kinetic = jnp.where(squared < radius, kinetic_scale * squared / radius, 0.0)
    lines_k = jnp.einsum("bacx,xrk->bacrk", orbitals, first_forward, precision=highest)
    along_f = jnp.einsum(
        "bacrk,crsf->baksf",
        lax.all_to_all(lines_k, "pencil", split_axis=4, concat_axis=2, tiled=True),
        second_forward,
        precision=highest,
    )
    spectra = jnp.einsum(
        "baksf,astg->bkftg",
        lax.all_to_all(along_f, "slab", split_axis=4, concat_axis=1, tiled=True),
        depth_forward,
        precision=highest,
    )
    spectra = spectra * kinetic[None, :, :, None, :]
    along_a = jnp.einsum("bkftg,gtsa->bkfsa", spectra, depth_inverse, precision=highest)
    returned = lax.all_to_all(along_a, "slab", split_axis=4, concat_axis=2, tiled=True)
    rows_c = jnp.einsum("bkfsa,fsrc->bkarc", returned, second_inverse, precision=highest)
    lines_x = lax.all_to_all(rows_c, "pencil", split_axis=4, concat_axis=1, tiled=True)
    kinetic_part = jnp.einsum("bkarc,krx->bacx", lines_x, first_inverse, precision=highest)
    kinetic_part = kinetic_part / float(NG**3)
    applied = kinetic_part + potential[None] * orbitals
    filtered = jnp.where(
        unlocked[:, None, None, None] == 1,
        (applied - filter_center * orbitals) / filter_half,
        orbitals,
    )
    number = filtered.shape[0]
    flattened = filtered.reshape(number, -1)
    partial_intersection = jnp.dot(flattened, flattened.T, precision=highest) / float(NG**3)
    intersection = lax.psum(partial_intersection, ("slab", "pencil"))
    factor = jnp.linalg.cholesky(intersection)
    result = jax.scipy.linalg.solve_triangular(factor, flattened, lower=True)
    return result.reshape(filtered.shape)


def solution(mesh):
    slabs, pencils = mesh.shape["slab"], mesh.shape["pencil"]

    def local(orbitals, potential, unlocked):
        bands, rows_a, rows_c, length = orbitals.shape
        half = length // 4
        f_block = 2 * half // pencils
        chunks = half // (2 * slabs)
        even = bands % 2 == 0 and bands // 2 * rows_c <= 128 and chunks > 0 and half % (2 * slabs) == 0
        fits = even and rows_a % 8 == 0 and rows_c % 8 == 0 and f_block % 8 == 0
        if fits:
            return by_kernel(slabs, pencils, chunks, orbitals, potential, unlocked)
        return by_collectives(orbitals, potential, unlocked)

    in_specs = (P(None, "slab", "pencil", None), P("slab", "pencil", None), P())
    out_specs = P(None, "slab", "pencil", None)
    return jax.shard_map(local, mesh=mesh, in_specs=in_specs, out_specs=out_specs, check_vma=False)
```

```python
import functools
import math

import jax
import jax.numpy as jnp
import ml_dtypes
import numpy as np
from jax import lax
from jax.experimental import pallas as pl
from jax.experimental.pallas import tpu as pltpu
from jax.sharding import PartitionSpec as P

MESH = pl.DeviceIdType.MESH


def dft_tables(length, slabs, pencils, chunks):
    half = length // 4
    pair = half // (slabs * chunks)
    place = np.arange(length)
    modes = np.arange(2 * half) - half
    third = np.arange(half)

    def waves(mode):
        angle = 2.0 * np.pi / length * ((mode[:, None] * place[None, :]) % length)
        return np.cos(angle), np.sin(angle)

    cos_k, sin_k = waves(third)
    weight = np.where(third == 0, 1.0, 2.0)[:, None]

    def order(cosine, sine):
        both = np.stack([cosine, sine], 0).reshape(2, chunks, slabs, pair, length)
        return both.transpose(1, 2, 0, 3, 4).reshape(2 * half, length)

    forward_x = order(cos_k, -sin_k).T
    inverse_x = order(weight * cos_k, -weight * sin_k)
    cosine, sine = waves(modes)
    forward = np.stack([np.stack([cosine, sine], 1), np.stack([-sine, cosine], 1)], 0)
    inverse = np.stack([np.stack([cosine.T, -sine.T], 1), np.stack([sine.T, cosine.T], 1)], 0)
    c_block = length // pencils
    forward_a = np.concatenate([cosine, sine], 0)
    forward_c = forward.reshape(4 * half, 2 * length).T
    inverse_c = inverse.reshape(2, pencils, c_block, 4 * half).transpose(1, 0, 2, 3).reshape(2 * length, 4 * half).T
    inverse_a = np.concatenate([cosine.T, sine.T], 0)
    tables = (forward_x, forward_a, forward_c, inverse_c, inverse_a, inverse_x)
    pairs = []
    for table in tables:
        high = table.astype(ml_dtypes.bfloat16)
        low = (table - high.astype(np.float64)).astype(ml_dtypes.bfloat16)
        pairs.append(np.stack([high, low], 0))
    return pairs


def split(value):
    high = value.astype(jnp.bfloat16)
    return high, (value - high.astype(jnp.float32)).astype(jnp.bfloat16)


def product(left, right):
    return jnp.dot(left, right, preferred_element_type=jnp.float32)


def from_left(table, value):
    high, low = split(value)
    return product(table[0], high) + (product(table[0], low) + product(table[1], high))


def from_right(value, table):
    high, low = split(value)
    return product(high, table[0]) + (product(low, table[0]) + product(high, table[1]))


def kernel(sizes, unlocked, given, given_potential, fx, fa, fc, ic, ia, ix, row_k, row_f, col_s, kept, solver,
           orbitals, potential, out, load, store, lines, s1, r1, s2, r2, s3, r3, s4, r4, back, sums, g1, h1, g2, h2,
           own, send1, recv1, send2, recv2, send3, recv3, send4, recv4, gs1, gr1, gs2, gr2):
    slabs, pencils, chunks, pair, bands, length = sizes
    few = bands // 2
    rows_a = orbitals.shape[1]
    rows_c = orbitals.shape[2]
    half = length // 4
    f_block = 2 * half // pencils
    wide = few * rows_c
    packed = 2 * pair * wide
    i_s = lax.axis_index("slab")
    i_p = lax.axis_index("pencil")

    def slab_peer(d):
        return lax.rem(i_s + d, slabs)

    def pencil_peer(d):
        return lax.rem(i_p + d, pencils)

    group = 8

    def fetch(h, g):
        at = (pl.ds(h * few, few), pl.ds(pl.multiple_of(g * group, group), group))
        return pltpu.make_async_copy(given.at[at], orbitals.at[at], load.at[h, g])

    fetch_potential = pltpu.make_async_copy(given_potential, potential, load.at[2, 0])
    for h in range(2):
        for g in range(rows_a // group):
            fetch(h, g).start()
    fetch_potential.start()

    def keep(h):
        return pltpu.make_async_copy(out.at[pl.ds(h * few, few)], kept.at[pl.ds(h * few, few)], store.at[h])

    barrier = pltpu.get_barrier_semaphore()
    for d in range(1, slabs):
        pl.semaphore_signal(barrier, inc=1, device_id=(slab_peer(d), i_p), device_id_type=MESH)
    for d in range(1, pencils):
        pl.semaphore_signal(barrier, inc=1, device_id=(i_s, pencil_peer(d)), device_id_type=MESH)

    def to_slab(d, src, dst, send, recv):
        return pltpu.make_async_remote_copy(
            src_ref=src, dst_ref=dst, send_sem=send, recv_sem=recv,
            device_id=(slab_peer(d), i_p), device_id_type=MESH)

    def to_pencil(d, src, dst, send, recv):
        return pltpu.make_async_remote_copy(
            src_ref=src, dst_ref=dst, send_sem=send, recv_sem=recv,
            device_id=(i_s, pencil_peer(d)), device_id_type=MESH)

    mine_a = pl.ds(pl.multiple_of(i_s * rows_a, 8), rows_a)
    mine_f = pl.ds(pl.multiple_of(i_p * f_block, 8), f_block)

    def copies(which, q):
        if which == 0:
            remote = [to_slab(d, s1.at[q, slab_peer(d)], r1.at[q, mine_a, :], send1.at[q, d], recv1.at[q, d])
                      for d in range(1, slabs)]
            local = pltpu.make_async_copy(s1.at[q, i_s], r1.at[q, mine_a, :], own.at[0, q])
        elif which == 1:
            remote = [to_pencil(d, s2.at[q, pencil_peer(d)], r2.at[q, i_p], send2.at[q, d], recv2.at[q, d])
                      for d in range(1, pencils)]
            local = pltpu.make_async_copy(s2.at[q, i_p], r2.at[q, i_p], own.at[1, q])
        elif which == 2:
            remote = [to_pencil(d, s3.at[q, pencil_peer(d)], r3.at[q, mine_f, :], send3.at[q, d], recv3.at[q, d])
                      for d in range(1, pencils)]
            local = pltpu.make_async_copy(s3.at[q, i_p], r3.at[q, mine_f, :], own.at[2, q])
        else:
            remote = [to_slab(d, s4.at[q, slab_peer(d)], r4.at[q, i_s], send4.at[q, d], recv4.at[q, d])
                      for d in range(1, slabs)]
            local = pltpu.make_async_copy(s4.at[q, i_s], r4.at[q, i_s], own.at[3, q])
        return remote, local

    def start(which, q):
        remote, local = copies(which, q)
        for copy in remote:
            copy.start()
        local.start()

    def arrived(which, q):
        remote, local = copies(which, q)
        for copy in remote:
            copy.wait_recv()
        local.wait()

    modes_x = 2 * half

    def forward_x(h):
        def body(g, carry):
            fetch(h, g).wait()
            rows = jnp.concatenate(
                [orbitals[h * few:(h + 1) * few, pl.ds(g * group + n, 1)].reshape(wide, length)
                 for n in range(group)], 0)
            result = from_right(rows, fx)
            for n in range(group):
                at = pl.multiple_of((g * group + n) * modes_x, modes_x)
                lines[h, pl.ds(at, modes_x), 0:wide] = result[n * wide:(n + 1) * wide].T
            return carry

        lax.fori_loop(0, rows_a // group, body, 0)

    def send_lines(h):
        for q in range(chunks):
            for j in range(slabs):
                s1[h * chunks + q, j] = jnp.concatenate(
                    [lines[h, pl.ds(((q * slabs + j) * 2 + r) * pair + k, rows_a, stride=modes_x), :][:, :wide]
                     for r in range(2) for k in range(pair)], 1)
            if h == 0:
                start(0, q)

    middle = packed // 2

    def first_forward(q):
        arrived(0, q)
        if q + chunks < 2 * chunks:
            start(0, q + chunks)
        result = from_left(fa, r1[q])
        cosine, sine = result[:2 * half], result[2 * half:]
        result = cosine + jnp.concatenate([sine[:, middle:], -sine[:, :middle]], 1)
        s2[q] = result.reshape(s2.shape[1:])
        start(1, q)

    def second(q):
        arrived(1, q)
        blocks = []
        for kb in range(pair * few):
            blocks.append(jnp.concatenate(
                [r2[q, p, :, r * middle + kb * rows_c:r * middle + (kb + 1) * rows_c]
                 for r in range(2) for p in range(pencils)], 1))
        spectrum = from_right(jnp.concatenate(blocks, 0), fc)
        mode_k = row_k[...] + (q % chunks * slabs * pair + i_s * pair).astype(jnp.float32)
        mode_f = row_f[...] + (i_p * f_block - half).astype(jnp.float32)
        squared = mode_k * mode_k + mode_f * mode_f + col_s[...]
        radius = float(half * half)
        kinetic = jnp.where(squared < radius, 4.0 * squared / radius, 0.0) * (1.0 / float(length**3))
        result = from_right(spectrum * kinetic, ic)
        for p in range(pencils):
            s3[q, p] = jnp.concatenate(
                [result[kb * f_block:(kb + 1) * f_block, (p * 2 + r) * rows_c:(p * 2 + r + 1) * rows_c]
                 for r in range(2) for kb in range(pair * few)], 1)
        start(2, q)

    def first_inverse(q):
        arrived(2, q)
        result = from_left(ia, r3[q])
        cosine, sine = result[:length], result[length:]
        result = cosine + jnp.concatenate([-sine[:, middle:], sine[:, :middle]], 1)
        s4[q] = result.reshape(s4.shape[1:])
        start(3, q)

    def take_lines(h, q):
        arrived(3, h * chunks + q)
        unused = jnp.zeros((rows_a, 128 - wide), jnp.float32)
        for j in range(slabs):
            value = r4[h * chunks + q, j]
            for r in range(2):
                for k in range(pair):
                    piece = value[:, r * middle + k * wide:r * middle + (k + 1) * wide]
                    back[h, pl.ds(((q * slabs + j) * 2 + r) * pair + k, rows_a, stride=modes_x), :] = (
                        jnp.concatenate([piece, unused], 1))

    def inverse_x(h):
        def body(g, carry):
            spectra = []
            for n in range(group):
                at = pl.multiple_of((g * group + n) * modes_x, modes_x)
                spectra.append(back[h, pl.ds(at, modes_x), 0:wide].T)
            kinetic_parts = from_right(jnp.concatenate(spectra, 0), ix)
            for n in range(group):
                a = g * group + n
                level = potential[pl.ds(a, 1)].reshape(rows_c, length)
                filtered = [out[b, pl.ds(a, 1)].reshape(rows_c, length) for b in range(h * few)]
                for b in range(few):
                    orbital = orbitals[h * few + b, pl.ds(a, 1)].reshape(rows_c, length)
                    kinetic_part = kinetic_parts[n * wide + b * rows_c:n * wide + (b + 1) * rows_c]
                    applied = kinetic_part + level * orbital
                    value = jnp.where(unlocked[h * few + b] == 1, (applied - orbital) / 1.5, orbital)
                    out[h * few + b, pl.ds(a, 1)] = value.reshape(1, rows_c, length)
                    filtered.append(value)
                for b in range(h * few, (h + 1) * few):
                    for e in range(b + 1):
                        squares = filtered[b] * filtered[e]
                        sums[b * (b + 1) // 2 + e] += squares.reshape(rows_c // 8, 8, length).sum(0)
            return carry

        lax.fori_loop(0, rows_a // group, body, 0)

    sums[...] = jnp.zeros_like(sums)
    forward_x(0)
    pl.semaphore_wait(barrier, slabs - 1 + pencils - 1)
    send_lines(0)
    forward_x(1)
    send_lines(1)
    last = 2 * chunks
    for step in range(last + 1):
        if step < last:
            first_forward(step)
        if step >= 1:
            second(step - 1)
        if step >= 2:
            first_inverse(step - 2)
    for q in range(chunks):
        take_lines(0, q)
    first_inverse(last - 1)
    fetch_potential.wait()
    inverse_x(0)
    keep(0).start()
    for q in range(chunks):
        take_lines(1, q)
    inverse_x(1)
    keep(1).start()

    total = jnp.sum(jnp.sum(sums[...], axis=1), axis=1, keepdims=True)
    g1[...] = jnp.broadcast_to(total, g1.shape)
    shares = [to_slab(d, g1, h1.at[i_s], gs1.at[d], gr1.at[d]) for d in range(1, slabs)]
    for copy in shares:
        copy.start()
    h1[pl.ds(i_s, 1)] = g1[...][None]
    for copy in shares:
        copy.wait()
    g2[...] = jnp.sum(h1[...], axis=0)
    shares = [to_pencil(d, g2, h2.at[i_p], gs2.at[d], gr2.at[d]) for d in range(1, pencils)]
    for copy in shares:
        copy.start()
    h2[pl.ds(i_p, 1)] = g2[...][None]
    for copy in shares:
        copy.wait()
    gram = jnp.sum(h2[...], axis=0) / float(length**3)

    factor = {}
    for b in range(bands):
        for e in range(b + 1):
            n = b * (b + 1) // 2 + e
            value = gram[n:n + 1, 0:1]
            for m in range(e):
                value = value - factor[b, m] * factor[e, m]
            factor[b, e] = jnp.sqrt(value) if b == e else value / factor[e, e]
    entries = [1.0 / factor[b, e] if b == e else factor[b, e] for b in range(bands) for e in range(b + 1)]
    for n, entry in enumerate(entries):
        solver[n:n + 1, :] = jnp.broadcast_to(entry, (1, 128))
    for h in range(2):
        keep(h).wait()
    for which in range(4):
        for q in range(2 * chunks):
            for copy in copies(which, q)[0]:
                copy.wait_send()


def solve(solver, filtered, out):
    bands, rows_a, rows_c, length = filtered.shape
    for a in range(rows_a):
        solved = []
        for b in range(bands):
            value = filtered[b, a]
            first = b * (b + 1) // 2
            for m in range(b):
                value = value - solver[first + m:first + m + 1, 0:1] * solved[m]
            value = value * solver[first + b:first + b + 1, 0:1]
            out[b, a] = value
            solved.append(value)


def by_kernel(slabs, pencils, chunks, orbitals, potential, unlocked):
    bands, rows_a, rows_c, length = orbitals.shape
    half = length // 4
    pair = half // (slabs * chunks)
    f_block = 2 * half // pencils
    few = bands // 2
    parts = 2 * chunks
    packed = 2 * pair * few * rows_c
    pairs = bands * (bands + 1) // 2
    tables = dft_tables(length, slabs, pencils, chunks)
    rows = np.arange(pair * few * f_block)
    row_k = (rows // (few * f_block)).astype(np.float32)[:, None]
    row_f = (rows % f_block).astype(np.float32)[:, None]
    col_s = ((np.arange(4 * half) % (2 * half) - half).astype(np.float32) ** 2)[None, :]
    vmem = pl.BlockSpec(memory_space=pltpu.VMEM)
    f32 = jnp.float32
    dma = pltpu.SemaphoreType.DMA
    scratch = [
        pltpu.VMEM(orbitals.shape, f32),
        pltpu.VMEM(potential.shape, f32),
        pltpu.VMEM(orbitals.shape, f32),
        dma((3, rows_a // 8)),
        dma((2,)),
        pltpu.VMEM((2, rows_a * 2 * half, 128), f32),
        pltpu.VMEM((parts, slabs, rows_a, packed), f32),
        pltpu.VMEM((parts, length, packed), f32),
        pltpu.VMEM((parts, pencils, f_block, packed), f32),
        pltpu.VMEM((parts, pencils, f_block, packed), f32),
        pltpu.VMEM((parts, pencils, f_block, packed), f32),
        pltpu.VMEM((parts, 2 * half, packed), f32),
        pltpu.VMEM((parts, slabs, rows_a, packed), f32),
        pltpu.VMEM((parts, slabs, rows_a, packed), f32),
        pltpu.VMEM((2, rows_a * 2 * half, 128), f32),
        pltpu.VMEM((pairs, 8, length), f32),
        pltpu.VMEM((pairs, 128), f32),
        pltpu.VMEM((slabs, pairs, 128), f32),
        pltpu.VMEM((pairs, 128), f32),
        pltpu.VMEM((pencils, pairs, 128), f32),
        dma((4, parts)),
        dma((parts, slabs)), dma((parts, slabs)),
        dma((parts, pencils)), dma((parts, pencils)),
        dma((parts, pencils)), dma((parts, pencils)),
        dma((parts, slabs)), dma((parts, slabs)),
        dma((slabs,)), dma((slabs,)),
        dma((pencils,)), dma((pencils,)),
    ]
    flops = 2 * rows_a * bands * rows_c * length * 2 * half * 6
    anywhere = pl.BlockSpec(memory_space=pl.ANY)
    filtered, solver = pl.pallas_call(
        functools.partial(kernel, (slabs, pencils, chunks, pair, bands, length)),
        out_shape=[jax.ShapeDtypeStruct(orbitals.shape, f32), jax.ShapeDtypeStruct((pairs, 128), f32)],
        in_specs=[pl.BlockSpec(memory_space=pltpu.SMEM), anywhere, anywhere] + [vmem] * 9,
        out_specs=[anywhere, vmem],
        scratch_shapes=scratch,
        compiler_params=pltpu.CompilerParams(
            collective_id=0, has_side_effects=True, vmem_limit_bytes=56 * 1024 * 1024),
        cost_estimate=pl.CostEstimate(flops=flops, bytes_accessed=10 * 2**20, transcendentals=0),
    )(unlocked, orbitals, potential, *[jnp.asarray(t) for t in tables],
      jnp.asarray(row_k), jnp.asarray(row_f), jnp.asarray(col_s))
    planes = 4
    block = pl.BlockSpec((bands, planes, rows_c, length), lambda i: (0, i, 0, 0))
    return pl.pallas_call(
        solve,
        grid=(rows_a // planes,),
        out_shape=jax.ShapeDtypeStruct(orbitals.shape, f32),
        in_specs=[pl.BlockSpec((pairs, 128), lambda i: (0, 0)), block],
        out_specs=block,
        cost_estimate=pl.CostEstimate(flops=20 * orbitals.size, bytes_accessed=8 * orbitals.size, transcendentals=0),
    )(solver, filtered)


NG = 192


kinetic_scale = 4.0
filter_center = 1.0
filter_half = 1.5
highest = lax.Precision.HIGHEST


def frequencies(number, length):
    index = jnp.arange(number, dtype=jnp.int32)
    if number == length:
        return jnp.where(index < length // 2, index, index - length)
    return index - length // 4


def tables(number, length):
    modes = frequencies(number, length)
    places = jnp.arange(length, dtype=jnp.int32)
    product = places[:, None] * modes[None, :] % length
    angle = 2.0 * math.pi / length * product.astype(jnp.float32)
    return (jnp.cos(angle), jnp.sin(angle))


def forward_table(cosine, sine):
    return jnp.stack([jnp.stack([cosine, -sine], 1), jnp.stack([sine, cosine], 1)], 1)


def inverse_table(cosine, sine):
    cos_t = cosine.T
    sin_t = sine.T
    return jnp.stack([jnp.stack([cos_t, sin_t], 1), jnp.stack([-sin_t, cos_t], 1)], 1)


def by_collectives(orbitals, potential, unlocked):
    length = orbitals.shape[3]
    kept_modes = length // 2
    cos_k, sin_k = tables(kept_modes, length)
    cos_f, sin_f = tables(length, length)
    first_forward = jnp.stack([cos_k, -sin_k], 1)
    first_inverse = jnp.stack([cos_k.T, -sin_k.T], 1)
    second_forward = forward_table(cos_k, sin_k)
    second_inverse = inverse_table(cos_k, sin_k)
    depth_forward = forward_table(cos_f, sin_f)
    depth_inverse = inverse_table(cos_f, sin_f)
    pencil_block = kept_modes // lax.axis_size("pencil")
    slab_block = kept_modes // lax.axis_size("slab")
    kept_list = frequencies(kept_modes, length)
    third_modes = lax.dynamic_slice_in_dim(
        kept_list, lax.axis_index("pencil") * pencil_block, pencil_block
    ).astype(jnp.float32)
    second_modes = lax.dynamic_slice_in_dim(
        kept_list, lax.axis_index("slab") * slab_block, slab_block
    ).astype(jnp.float32)
    first_modes = frequencies(length, length).astype(jnp.float32)
    squared = (
        third_modes[:, None, None] ** 2
        + second_modes[None, :, None] ** 2
        + first_modes[None, None, :] ** 2
    )
    radius = float((length // 4) ** 2)
    kinetic = jnp.where(squared < radius, kinetic_scale * squared / radius, 0.0)
    lines_k = jnp.einsum("bacx,xrk->bacrk", orbitals, first_forward, precision=highest)
    along_f = jnp.einsum(
        "bacrk,crsf->baksf",
        lax.all_to_all(lines_k, "pencil", split_axis=4, concat_axis=2, tiled=True),
        second_forward,
        precision=highest,
    )
    spectra = jnp.einsum(
        "baksf,astg->bkftg",
        lax.all_to_all(along_f, "slab", split_axis=4, concat_axis=1, tiled=True),
        depth_forward,
        precision=highest,
    )
    spectra = spectra * kinetic[None, :, :, None, :]
    along_a = jnp.einsum("bkftg,gtsa->bkfsa", spectra, depth_inverse, precision=highest)
    returned = lax.all_to_all(along_a, "slab", split_axis=4, concat_axis=2, tiled=True)
    rows_c = jnp.einsum("bkfsa,fsrc->bkarc", returned, second_inverse, precision=highest)
    lines_x = lax.all_to_all(rows_c, "pencil", split_axis=4, concat_axis=1, tiled=True)
    kinetic_part = jnp.einsum("bkarc,krx->bacx", lines_x, first_inverse, precision=highest)
    kinetic_part = kinetic_part / float(NG**3)
    applied = kinetic_part + potential[None] * orbitals
    filtered = jnp.where(
        unlocked[:, None, None, None] == 1,
        (applied - filter_center * orbitals) / filter_half,
        orbitals,
    )
    number = filtered.shape[0]
    flattened = filtered.reshape(number, -1)
    partial_intersection = jnp.dot(flattened, flattened.T, precision=highest) / float(NG**3)
    intersection = lax.psum(partial_intersection, ("slab", "pencil"))
    factor = jnp.linalg.cholesky(intersection)
    result = jax.scipy.linalg.solve_triangular(factor, flattened, lower=True)
    return result.reshape(filtered.shape)


def solution(mesh):
    slabs, pencils = mesh.shape["slab"], mesh.shape["pencil"]

    def local(orbitals, potential, unlocked):
        bands, rows_a, rows_c, length = orbitals.shape
        half = length // 4
        f_block = 2 * half // pencils
        chunks = half // (2 * slabs)
        even = bands % 2 == 0 and bands // 2 * rows_c <= 128 and chunks > 0 and half % (2 * slabs) == 0
        fits = even and rows_a % 8 == 0 and rows_c % 8 == 0 and f_block % 8 == 0
        if fits:
            return by_kernel(slabs, pencils, chunks, orbitals, potential, unlocked)
        return by_collectives(orbitals, potential, unlocked)

    in_specs = (P(None, "slab", "pencil", None), P("slab", "pencil", None), P())
    out_specs = P(None, "slab", "pencil", None)
    return jax.shard_map(local, mesh=mesh, in_specs=in_specs, out_specs=out_specs, check_vma=False)
```

```python
import functools
import math

import jax
import jax.numpy as jnp
import ml_dtypes
import numpy as np
from jax import lax
from jax.experimental import pallas as pl
from jax.experimental.pallas import tpu as pltpu
from jax.sharding import PartitionSpec as P

MESH = pl.DeviceIdType.MESH


def dft_tables(length, slabs, pencils, chunks):
    half = length // 4
    pair = half // (slabs * chunks)
    place = np.arange(length)
    modes = np.arange(2 * half) - half
    third = np.arange(half)

    def waves(mode):
        angle = 2.0 * np.pi / length * ((mode[:, None] * place[None, :]) % length)
        return np.cos(angle), np.sin(angle)

    cos_k, sin_k = waves(third)
    weight = np.where(third == 0, 1.0, 2.0)[:, None]

    def order(cosine, sine):
        both = np.stack([cosine, sine], 0).reshape(2, chunks, slabs, pair, length)
        return both.transpose(1, 2, 0, 3, 4).reshape(2 * half, length)

    forward_x = order(cos_k, -sin_k).T
    inverse_x = order(weight * cos_k, -weight * sin_k)
    cosine, sine = waves(modes)
    forward = np.stack([np.stack([cosine, sine], 1), np.stack([-sine, cosine], 1)], 0)
    inverse = np.stack([np.stack([cosine.T, -sine.T], 1), np.stack([sine.T, cosine.T], 1)], 0)
    c_block = length // pencils
    forward_a = np.concatenate([cosine, sine], 0)
    forward_c = forward.reshape(4 * half, 2 * length).T
    inverse_c = inverse.reshape(2, pencils, c_block, 4 * half).transpose(1, 0, 2, 3).reshape(2 * length, 4 * half).T
    inverse_a = np.concatenate([cosine.T, sine.T], 0)
    tables = (forward_x, forward_a, forward_c, inverse_c, inverse_a, inverse_x)
    pairs = []
    for table in tables:
        high = table.astype(ml_dtypes.bfloat16)
        low = (table - high.astype(np.float64)).astype(ml_dtypes.bfloat16)
        pairs.append(np.stack([high, low], 0))
    return pairs


def split(value):
    high = value.astype(jnp.bfloat16)
    return high, (value - high.astype(jnp.float32)).astype(jnp.bfloat16)


def product(left, right):
    return jnp.dot(left, right, preferred_element_type=jnp.float32)


def from_left(table, value):
    high, low = split(value)
    return product(table[0], high) + (product(table[0], low) + product(table[1], high))


def from_right(value, table):
    high, low = split(value)
    return product(high, table[0]) + (product(low, table[0]) + product(high, table[1]))


def kernel(sizes, unlocked, given, given_potential, fx, fa, fc, ic, ia, ix, row_k, row_f, col_s, kept, solver,
           orbitals, potential, out, load, store, lines, s1, r1, s2, r2, s3, r3, s4, r4, back, sums, g1, h1, g2, h2,
           own, send1, recv1, send2, recv2, send3, recv3, send4, recv4, gs1, gr1, gs2, gr2):
    slabs, pencils, chunks, pair, bands, length = sizes
    few = bands // 2
    rows_a = orbitals.shape[1]
    rows_c = orbitals.shape[2]
    half = length // 4
    f_block = 2 * half // pencils
    wide = few * rows_c
    packed = 2 * pair * wide
    i_s = lax.axis_index("slab")
    i_p = lax.axis_index("pencil")

    def slab_peer(d):
        return lax.rem(i_s + d, slabs)

    def pencil_peer(d):
        return lax.rem(i_p + d, pencils)

    group = 8

    def fetch(h, g):
        at = (pl.ds(h * few, few), pl.ds(pl.multiple_of(g * group, group), group))
        return pltpu.make_async_copy(given.at[at], orbitals.at[at], load.at[h, g])

    fetch_potential = pltpu.make_async_copy(given_potential, potential, load.at[2, 0])
    for h in range(2):
        for g in range(rows_a // group):
            fetch(h, g).start()
    fetch_potential.start()

    def keep(h):
        return pltpu.make_async_copy(out.at[pl.ds(h * few, few)], kept.at[pl.ds(h * few, few)], store.at[h])

    barrier = pltpu.get_barrier_semaphore()
    for d in range(1, slabs):
        pl.semaphore_signal(barrier, inc=1, device_id=(slab_peer(d), i_p), device_id_type=MESH)
    for d in range(1, pencils):
        pl.semaphore_signal(barrier, inc=1, device_id=(i_s, pencil_peer(d)), device_id_type=MESH)

    def to_slab(d, src, dst, send, recv):
        return pltpu.make_async_remote_copy(
            src_ref=src, dst_ref=dst, send_sem=send, recv_sem=recv,
            device_id=(slab_peer(d), i_p), device_id_type=MESH)

    def to_pencil(d, src, dst, send, recv):
        return pltpu.make_async_remote_copy(
            src_ref=src, dst_ref=dst, send_sem=send, recv_sem=recv,
            device_id=(i_s, pencil_peer(d)), device_id_type=MESH)

    mine_a = pl.ds(pl.multiple_of(i_s * rows_a, 8), rows_a)
    mine_f = pl.ds(pl.multiple_of(i_p * f_block, 8), f_block)

    def copies(which, q):
        if which == 0:
            remote = [to_slab(d, s1.at[q, slab_peer(d)], r1.at[q, mine_a, :], send1.at[q, d], recv1.at[q, d])
                      for d in range(1, slabs)]
            local = pltpu.make_async_copy(s1.at[q, i_s], r1.at[q, mine_a, :], own.at[0, q])
        elif which == 1:
            remote = [to_pencil(d, s2.at[q, pencil_peer(d)], r2.at[q, i_p], send2.at[q, d], recv2.at[q, d])
                      for d in range(1, pencils)]
            local = pltpu.make_async_copy(s2.at[q, i_p], r2.at[q, i_p], own.at[1, q])
        elif which == 2:
            remote = [to_pencil(d, s3.at[q, pencil_peer(d)], r3.at[q, mine_f, :], send3.at[q, d], recv3.at[q, d])
                      for d in range(1, pencils)]
            local = pltpu.make_async_copy(s3.at[q, i_p], r3.at[q, mine_f, :], own.at[2, q])
        else:
            remote = [to_slab(d, s4.at[q, slab_peer(d)], r4.at[q, i_s], send4.at[q, d], recv4.at[q, d])
                      for d in range(1, slabs)]
            local = pltpu.make_async_copy(s4.at[q, i_s], r4.at[q, i_s], own.at[3, q])
        return remote, local

    def start(which, q):
        remote, local = copies(which, q)
        for copy in remote:
            copy.start()
        local.start()

    def arrived(which, q):
        remote, local = copies(which, q)
        for copy in remote:
            copy.wait_recv()
        local.wait()

    modes_x = 2 * half

    def forward_x(h):
        def body(g, carry):
            fetch(h, g).wait()
            rows = jnp.concatenate(
                [orbitals[h * few:(h + 1) * few, pl.ds(g * group + n, 1)].reshape(wide, length)
                 for n in range(group)], 0)
            result = from_right(rows, fx)
            for n in range(group):
                at = pl.multiple_of((g * group + n) * modes_x, modes_x)
                lines[h, pl.ds(at, modes_x), 0:wide] = result[n * wide:(n + 1) * wide].T
            return carry

        lax.fori_loop(0, rows_a // group, body, 0)

    def send_lines(h, q):
        for j in range(slabs):
            s1[h * chunks + q, j] = jnp.concatenate(
                [lines[h, pl.ds(((q * slabs + j) * 2 + r) * pair + k, rows_a, stride=modes_x), :][:, :wide]
                 for r in range(2) for k in range(pair)], 1)
        start(0, h * chunks + q)

    middle = packed // 2

    def first_forward(q):
        arrived(0, q)
        result = from_left(fa, r1[q])
        cosine, sine = result[:2 * half], result[2 * half:]
        result = cosine + jnp.concatenate([sine[:, middle:], -sine[:, :middle]], 1)
        s2[q] = result.reshape(s2.shape[1:])
        start(1, q)
        if q < chunks:
            send_lines(1, q)

    def second(q):
        arrived(1, q)
        blocks = []
        for kb in range(pair * few):
            blocks.append(jnp.concatenate(
                [r2[q, p, :, r * middle + kb * rows_c:r * middle + (kb + 1) * rows_c]
                 for r in range(2) for p in range(pencils)], 1))
        spectrum = from_right(jnp.concatenate(blocks, 0), fc)
        mode_k = row_k[...] + (q % chunks * slabs * pair + i_s * pair).astype(jnp.float32)
        mode_f = row_f[...] + (i_p * f_block - half).astype(jnp.float32)
        squared = mode_k * mode_k + mode_f * mode_f + col_s[...]
        radius = float(half * half)
        kinetic = jnp.where(squared < radius, 4.0 * squared / radius, 0.0) * (1.0 / float(length**3))
        result = from_right(spectrum * kinetic, ic)
        for p in range(pencils):
            s3[q, p] = jnp.concatenate(
                [result[kb * f_block:(kb + 1) * f_block, (p * 2 + r) * rows_c:(p * 2 + r + 1) * rows_c]
                 for r in range(2) for kb in range(pair * few)], 1)
        start(2, q)

    def first_inverse(q):
        arrived(2, q)
        result = from_left(ia, r3[q])
        cosine, sine = result[:length], result[length:]
        result = cosine + jnp.concatenate([-sine[:, middle:], sine[:, :middle]], 1)
        s4[q] = result.reshape(s4.shape[1:])
        start(3, q)

    def take_lines(h, q):
        arrived(3, h * chunks + q)
        unused = jnp.zeros((rows_a, 128 - wide), jnp.float32)
        for j in range(slabs):
            value = r4[h * chunks + q, j]
            for r in range(2):
                for k in range(pair):
                    piece = value[:, r * middle + k * wide:r * middle + (k + 1) * wide]
                    back[h, pl.ds(((q * slabs + j) * 2 + r) * pair + k, rows_a, stride=modes_x), :] = (
                        jnp.concatenate([piece, unused], 1))

    def inverse_x(h, first, end):
        def body(g, carry):
            spectra = []
            for n in range(group):
                at = pl.multiple_of((g * group + n) * modes_x, modes_x)
                spectra.append(back[h, pl.ds(at, modes_x), 0:wide].T)
            kinetic_parts = from_right(jnp.concatenate(spectra, 0), ix)
            for n in range(group):
                a = g * group + n
                level = potential[pl.ds(a, 1)].reshape(rows_c, length)
                filtered = [out[b, pl.ds(a, 1)].reshape(rows_c, length) for b in range(h * few)]
                for b in range(few):
                    orbital = orbitals[h * few + b, pl.ds(a, 1)].reshape(rows_c, length)
                    kinetic_part = kinetic_parts[n * wide + b * rows_c:n * wide + (b + 1) * rows_c]
                    applied = kinetic_part + level * orbital
                    value = jnp.where(unlocked[h * few + b] == 1, (applied - orbital) / 1.5, orbital)
                    out[h * few + b, pl.ds(a, 1)] = value.reshape(1, rows_c, length)
                    filtered.append(value)
                for b in range(h * few, (h + 1) * few):
                    for e in range(b + 1):
                        squares = filtered[b] * filtered[e]
                        sums[b * (b + 1) // 2 + e] += squares.reshape(rows_c // 8, 8, length).sum(0)
            return carry

        lax.fori_loop(first, end, body, 0)

    sums[...] = jnp.zeros_like(sums)
    forward_x(0)
    pl.semaphore_wait(barrier, slabs - 1 + pencils - 1)
    for q in range(chunks):
        send_lines(0, q)
    forward_x(1)
    last = 2 * chunks
    for step in range(last + 1):
        if step < last:
            first_forward(step)
        if step >= 1:
            second(step - 1)
        if step >= 2:
            first_inverse(step - 2)
        if step >= last - 1:
            for q in range(chunks - 1) if step < last else range(chunks - 1, chunks):
                take_lines(0, q)
    groups = rows_a // group
    early = groups - groups // 3
    fetch_potential.wait()
    inverse_x(0, 0, early)
    first_inverse(last - 1)
    inverse_x(0, early, groups)
    keep(0).start()
    for q in range(chunks):
        take_lines(1, q)
    inverse_x(1, 0, groups)
    keep(1).start()

    total = jnp.sum(jnp.sum(sums[...], axis=1), axis=1, keepdims=True)
    g1[...] = jnp.broadcast_to(total, g1.shape)
    shares = [to_slab(d, g1, h1.at[i_s], gs1.at[d], gr1.at[d]) for d in range(1, slabs)]
    for copy in shares:
        copy.start()
    h1[pl.ds(i_s, 1)] = g1[...][None]
    for copy in shares:
        copy.wait()
    g2[...] = jnp.sum(h1[...], axis=0)
    shares = [to_pencil(d, g2, h2.at[i_p], gs2.at[d], gr2.at[d]) for d in range(1, pencils)]
    for copy in shares:
        copy.start()
    h2[pl.ds(i_p, 1)] = g2[...][None]
    for copy in shares:
        copy.wait()
    gram = jnp.sum(h2[...], axis=0) / float(length**3)

    factor = {}
    for b in range(bands):
        for e in range(b + 1):
            n = b * (b + 1) // 2 + e
            value = gram[n:n + 1, 0:1]
            for m in range(e):
                value = value - factor[b, m] * factor[e, m]
            factor[b, e] = jnp.sqrt(value) if b == e else value / factor[e, e]
    entries = [1.0 / factor[b, e] if b == e else factor[b, e] for b in range(bands) for e in range(b + 1)]
    for n, entry in enumerate(entries):
        solver[n:n + 1, :] = jnp.broadcast_to(entry, (1, 128))
    for h in range(2):
        keep(h).wait()
    for which in range(4):
        for q in range(2 * chunks):
            for copy in copies(which, q)[0]:
                copy.wait_send()


def solve(solver, filtered, out):
    bands, rows_a, rows_c, length = filtered.shape
    for a in range(rows_a):
        solved = []
        for b in range(bands):
            value = filtered[b, a]
            first = b * (b + 1) // 2
            for m in range(b):
                value = value - solver[first + m, 0] * solved[m]
            value = value * solver[first + b, 0]
            out[b, a] = value
            solved.append(value)


def by_kernel(slabs, pencils, chunks, orbitals, potential, unlocked):
    bands, rows_a, rows_c, length = orbitals.shape
    half = length // 4
    pair = half // (slabs * chunks)
    f_block = 2 * half // pencils
    few = bands // 2
    parts = 2 * chunks
    packed = 2 * pair * few * rows_c
    pairs = bands * (bands + 1) // 2
    tables = dft_tables(length, slabs, pencils, chunks)
    rows = np.arange(pair * few * f_block)
    row_k = (rows // (few * f_block)).astype(np.float32)[:, None]
    row_f = (rows % f_block).astype(np.float32)[:, None]
    col_s = ((np.arange(4 * half) % (2 * half) - half).astype(np.float32) ** 2)[None, :]
    vmem = pl.BlockSpec(memory_space=pltpu.VMEM)
    f32 = jnp.float32
    dma = pltpu.SemaphoreType.DMA
    scratch = [
        pltpu.VMEM(orbitals.shape, f32),
        pltpu.VMEM(potential.shape, f32),
        pltpu.VMEM(orbitals.shape, f32),
        dma((3, rows_a // 8)),
        dma((2,)),
        pltpu.VMEM((2, rows_a * 2 * half, 128), f32),
        pltpu.VMEM((parts, slabs, rows_a, packed), f32),
        pltpu.VMEM((parts, length, packed), f32),
        pltpu.VMEM((parts, pencils, f_block, packed), f32),
        pltpu.VMEM((parts, pencils, f_block, packed), f32),
        pltpu.VMEM((parts, pencils, f_block, packed), f32),
        pltpu.VMEM((parts, 2 * half, packed), f32),
        pltpu.VMEM((parts, slabs, rows_a, packed), f32),
        pltpu.VMEM((parts, slabs, rows_a, packed), f32),
        pltpu.VMEM((2, rows_a * 2 * half, 128), f32),
        pltpu.VMEM((pairs, 8, length), f32),
        pltpu.VMEM((pairs, 128), f32),
        pltpu.VMEM((slabs, pairs, 128), f32),
        pltpu.VMEM((pairs, 128), f32),
        pltpu.VMEM((pencils, pairs, 128), f32),
        dma((4, parts)),
        dma((parts, slabs)), dma((parts, slabs)),
        dma((parts, pencils)), dma((parts, pencils)),
        dma((parts, pencils)), dma((parts, pencils)),
        dma((parts, slabs)), dma((parts, slabs)),
        dma((slabs,)), dma((slabs,)),
        dma((pencils,)), dma((pencils,)),
    ]
    flops = 2 * rows_a * bands * rows_c * length * 2 * half * 6
    anywhere = pl.BlockSpec(memory_space=pl.ANY)
    filtered, solver = pl.pallas_call(
        functools.partial(kernel, (slabs, pencils, chunks, pair, bands, length)),
        out_shape=[jax.ShapeDtypeStruct(orbitals.shape, f32), jax.ShapeDtypeStruct((pairs, 128), f32)],
        in_specs=[pl.BlockSpec(memory_space=pltpu.SMEM), anywhere, anywhere] + [vmem] * 9,
        out_specs=[anywhere, vmem],
        scratch_shapes=scratch,
        compiler_params=pltpu.CompilerParams(
            collective_id=0, has_side_effects=True, vmem_limit_bytes=56 * 1024 * 1024),
        cost_estimate=pl.CostEstimate(flops=flops, bytes_accessed=10 * 2**20, transcendentals=0),
    )(unlocked, orbitals, potential, *[jnp.asarray(t) for t in tables],
      jnp.asarray(row_k), jnp.asarray(row_f), jnp.asarray(col_s))
    planes = 4
    block = pl.BlockSpec((bands, planes, rows_c, length), lambda i: (0, i, 0, 0))
    return pl.pallas_call(
        solve,
        grid=(rows_a // planes,),
        out_shape=jax.ShapeDtypeStruct(orbitals.shape, f32),
        in_specs=[pl.BlockSpec(memory_space=pltpu.SMEM), block],
        out_specs=block,
        cost_estimate=pl.CostEstimate(flops=20 * orbitals.size, bytes_accessed=8 * orbitals.size, transcendentals=0),
    )(solver, filtered)


NG = 192


kinetic_scale = 4.0
filter_center = 1.0
filter_half = 1.5
highest = lax.Precision.HIGHEST


def frequencies(number, length):
    index = jnp.arange(number, dtype=jnp.int32)
    if number == length:
        return jnp.where(index < length // 2, index, index - length)
    return index - length // 4


def tables(number, length):
    modes = frequencies(number, length)
    places = jnp.arange(length, dtype=jnp.int32)
    product = places[:, None] * modes[None, :] % length
    angle = 2.0 * math.pi / length * product.astype(jnp.float32)
    return (jnp.cos(angle), jnp.sin(angle))


def forward_table(cosine, sine):
    return jnp.stack([jnp.stack([cosine, -sine], 1), jnp.stack([sine, cosine], 1)], 1)


def inverse_table(cosine, sine):
    cos_t = cosine.T
    sin_t = sine.T
    return jnp.stack([jnp.stack([cos_t, sin_t], 1), jnp.stack([-sin_t, cos_t], 1)], 1)


def by_collectives(orbitals, potential, unlocked):
    length = orbitals.shape[3]
    kept_modes = length // 2
    cos_k, sin_k = tables(kept_modes, length)
    cos_f, sin_f = tables(length, length)
    first_forward = jnp.stack([cos_k, -sin_k], 1)
    first_inverse = jnp.stack([cos_k.T, -sin_k.T], 1)
    second_forward = forward_table(cos_k, sin_k)
    second_inverse = inverse_table(cos_k, sin_k)
    depth_forward = forward_table(cos_f, sin_f)
    depth_inverse = inverse_table(cos_f, sin_f)
    pencil_block = kept_modes // lax.axis_size("pencil")
    slab_block = kept_modes // lax.axis_size("slab")
    kept_list = frequencies(kept_modes, length)
    third_modes = lax.dynamic_slice_in_dim(
        kept_list, lax.axis_index("pencil") * pencil_block, pencil_block
    ).astype(jnp.float32)
    second_modes = lax.dynamic_slice_in_dim(
        kept_list, lax.axis_index("slab") * slab_block, slab_block
    ).astype(jnp.float32)
    first_modes = frequencies(length, length).astype(jnp.float32)
    squared = (
        third_modes[:, None, None] ** 2
        + second_modes[None, :, None] ** 2
        + first_modes[None, None, :] ** 2
    )
    radius = float((length // 4) ** 2)
    kinetic = jnp.where(squared < radius, kinetic_scale * squared / radius, 0.0)
    lines_k = jnp.einsum("bacx,xrk->bacrk", orbitals, first_forward, precision=highest)
    along_f = jnp.einsum(
        "bacrk,crsf->baksf",
        lax.all_to_all(lines_k, "pencil", split_axis=4, concat_axis=2, tiled=True),
        second_forward,
        precision=highest,
    )
    spectra = jnp.einsum(
        "baksf,astg->bkftg",
        lax.all_to_all(along_f, "slab", split_axis=4, concat_axis=1, tiled=True),
        depth_forward,
        precision=highest,
    )
    spectra = spectra * kinetic[None, :, :, None, :]
    along_a = jnp.einsum("bkftg,gtsa->bkfsa", spectra, depth_inverse, precision=highest)
    returned = lax.all_to_all(along_a, "slab", split_axis=4, concat_axis=2, tiled=True)
    rows_c = jnp.einsum("bkfsa,fsrc->bkarc", returned, second_inverse, precision=highest)
    lines_x = lax.all_to_all(rows_c, "pencil", split_axis=4, concat_axis=1, tiled=True)
    kinetic_part = jnp.einsum("bkarc,krx->bacx", lines_x, first_inverse, precision=highest)
    kinetic_part = kinetic_part / float(NG**3)
    applied = kinetic_part + potential[None] * orbitals
    filtered = jnp.where(
        unlocked[:, None, None, None] == 1,
        (applied - filter_center * orbitals) / filter_half,
        orbitals,
    )
    number = filtered.shape[0]
    flattened = filtered.reshape(number, -1)
    partial_intersection = jnp.dot(flattened, flattened.T, precision=highest) / float(NG**3)
    intersection = lax.psum(partial_intersection, ("slab", "pencil"))
    factor = jnp.linalg.cholesky(intersection)
    result = jax.scipy.linalg.solve_triangular(factor, flattened, lower=True)
    return result.reshape(filtered.shape)


def solution(mesh):
    slabs, pencils = mesh.shape["slab"], mesh.shape["pencil"]

    def local(orbitals, potential, unlocked):
        bands, rows_a, rows_c, length = orbitals.shape
        half = length // 4
        f_block = 2 * half // pencils
        chunks = half // (2 * slabs)
        even = bands % 2 == 0 and bands // 2 * rows_c <= 128 and chunks > 0 and half % (2 * slabs) == 0
        fits = even and rows_a % 8 == 0 and rows_c % 8 == 0 and f_block % 8 == 0
        if fits:
            return by_kernel(slabs, pencils, chunks, orbitals, potential, unlocked)
        return by_collectives(orbitals, potential, unlocked)

    in_specs = (P(None, "slab", "pencil", None), P("slab", "pencil", None), P())
    out_specs = P(None, "slab", "pencil", None)
    return jax.shard_map(local, mesh=mesh, in_specs=in_specs, out_specs=out_specs, check_vma=False)
```

```python
import functools
import math

import jax
import jax.numpy as jnp
import ml_dtypes
import numpy as np
from jax import lax
from jax.experimental import pallas as pl
from jax.experimental.pallas import tpu as pltpu
from jax.sharding import PartitionSpec as P

MESH = pl.DeviceIdType.MESH


def dft_tables(length, slabs, pencils, chunks):
    half = length // 4
    pair = half // (slabs * chunks)
    place = np.arange(length)
    modes = np.arange(2 * half) - half
    third = np.arange(half)

    def waves(mode):
        angle = 2.0 * np.pi / length * ((mode[:, None] * place[None, :]) % length)
        return np.cos(angle), np.sin(angle)

    cos_k, sin_k = waves(third)
    weight = np.where(third == 0, 1.0, 2.0)[:, None]

    def order(cosine, sine):
        both = np.stack([cosine, sine], 0).reshape(2, chunks, slabs, pair, length)
        return both.transpose(1, 2, 0, 3, 4).reshape(2 * half, length)

    forward_x = order(cos_k, -sin_k).T
    inverse_x = order(weight * cos_k, -weight * sin_k)
    cosine, sine = waves(modes)
    forward = np.stack([np.stack([cosine, sine], 1), np.stack([-sine, cosine], 1)], 0)
    inverse = np.stack([np.stack([cosine.T, -sine.T], 1), np.stack([sine.T, cosine.T], 1)], 0)
    c_block = length // pencils
    forward_a = np.concatenate([cosine, sine], 0)
    forward_c = forward.reshape(4 * half, 2 * length).T
    inverse_c = inverse.reshape(2, pencils, c_block, 4 * half).transpose(1, 0, 2, 3).reshape(2 * length, 4 * half).T
    inverse_a = np.concatenate([cosine.T, sine.T], 0)
    tables = (forward_x, forward_a, forward_c, inverse_c, inverse_a, inverse_x)
    pairs = []
    for table in tables:
        high = table.astype(ml_dtypes.bfloat16)
        low = (table - high.astype(np.float64)).astype(ml_dtypes.bfloat16)
        pairs.append(np.stack([high, low], 0))
    return pairs


def split(value):
    high = value.astype(jnp.bfloat16)
    return high, (value - high.astype(jnp.float32)).astype(jnp.bfloat16)


def product(left, right):
    return jnp.dot(left, right, preferred_element_type=jnp.float32)


def from_left(table, value):
    high, low = split(value)
    return product(table[0], high) + (product(table[0], low) + product(table[1], high))


def from_right(value, table):
    high, low = split(value)
    return product(high, table[0]) + (product(low, table[0]) + product(high, table[1]))


def kernel(sizes, unlocked, given, given_potential, fx, fa, fc, ic, ia, ix, row_k, row_f, col_s, kept, solver,
           orbitals, potential, out, load, store, lines, s1, r1, s2, r2, s3, r3, s4, r4, back, sums, g1, h1, g2, h2,
           own, send1, recv1, send2, recv2, send3, recv3, send4, recv4, gs1, gr1, gs2, gr2):
    slabs, pencils, chunks, pair, bands, length = sizes
    few = bands // 2
    rows_a = orbitals.shape[1]
    rows_c = orbitals.shape[2]
    half = length // 4
    f_block = 2 * half // pencils
    wide = few * rows_c
    packed = 2 * pair * wide
    i_s = lax.axis_index("slab")
    i_p = lax.axis_index("pencil")

    def slab_peer(d):
        return lax.rem(i_s + d, slabs)

    def pencil_peer(d):
        return lax.rem(i_p + d, pencils)

    group = 8

    def fetch(h, g):
        at = (pl.ds(h * few, few), pl.ds(pl.multiple_of(g * group, group), group))
        return pltpu.make_async_copy(given.at[at], orbitals.at[at], load.at[h, g])

    fetch_potential = pltpu.make_async_copy(given_potential, potential, load.at[2, 0])
    for h in range(2):
        for g in range(rows_a // group):
            fetch(h, g).start()
    fetch_potential.start()

    def keep(h):
        return pltpu.make_async_copy(out.at[pl.ds(h * few, few)], kept.at[pl.ds(h * few, few)], store.at[h])

    barrier = pltpu.get_barrier_semaphore()
    for d in range(1, slabs):
        pl.semaphore_signal(barrier, inc=1, device_id=(slab_peer(d), i_p), device_id_type=MESH)
    for d in range(1, pencils):
        pl.semaphore_signal(barrier, inc=1, device_id=(i_s, pencil_peer(d)), device_id_type=MESH)

    def to_slab(d, src, dst, send, recv):
        return pltpu.make_async_remote_copy(
            src_ref=src, dst_ref=dst, send_sem=send, recv_sem=recv,
            device_id=(slab_peer(d), i_p), device_id_type=MESH)

    def to_pencil(d, src, dst, send, recv):
        return pltpu.make_async_remote_copy(
            src_ref=src, dst_ref=dst, send_sem=send, recv_sem=recv,
            device_id=(i_s, pencil_peer(d)), device_id_type=MESH)

    mine_a = pl.ds(pl.multiple_of(i_s * rows_a, 8), rows_a)
    mine_f = pl.ds(pl.multiple_of(i_p * f_block, 8), f_block)

    def copies(which, q):
        if which == 0:
            remote = [to_slab(d, s1.at[q, slab_peer(d)], r1.at[q, mine_a, :], send1.at[q, d], recv1.at[q, d])
                      for d in range(1, slabs)]
            local = pltpu.make_async_copy(s1.at[q, i_s], r1.at[q, mine_a, :], own.at[0, q])
        elif which == 1:
            remote = [to_pencil(d, s2.at[q, pencil_peer(d)], r2.at[q, i_p], send2.at[q, d], recv2.at[q, d])
                      for d in range(1, pencils)]
            local = pltpu.make_async_copy(s2.at[q, i_p], r2.at[q, i_p], own.at[1, q])
        elif which == 2:
            remote = [to_pencil(d, s3.at[q, pencil_peer(d)], r3.at[q, mine_f, :], send3.at[q, d], recv3.at[q, d])
                      for d in range(1, pencils)]
            local = pltpu.make_async_copy(s3.at[q, i_p], r3.at[q, mine_f, :], own.at[2, q])
        else:
            remote = [to_slab(d, s4.at[q, slab_peer(d)], r4.at[q, i_s], send4.at[q, d], recv4.at[q, d])
                      for d in range(1, slabs)]
            local = pltpu.make_async_copy(s4.at[q, i_s], r4.at[q, i_s], own.at[3, q])
        return remote, local

    def start(which, q):
        remote, local = copies(which, q)
        for copy in remote:
            copy.start()
        local.start()

    def arrived(which, q):
        remote, local = copies(which, q)
        for copy in remote:
            copy.wait_recv()
        local.wait()

    modes_x = 2 * half

    def forward_x(h):
        def body(g, carry):
            fetch(h, g).wait()
            rows = jnp.concatenate(
                [orbitals[h * few:(h + 1) * few, pl.ds(g * group + n, 1)].reshape(wide, length)
                 for n in range(group)], 0)
            result = from_right(rows, fx)
            for n in range(group):
                at = pl.multiple_of((g * group + n) * modes_x, modes_x)
                lines[h, pl.ds(at, modes_x), 0:wide] = result[n * wide:(n + 1) * wide].T
            return carry

        lax.fori_loop(0, rows_a // group, body, 0)

    def send_lines(h, q):
        for j in range(slabs):
            s1[h * chunks + q, j] = jnp.concatenate(
                [lines[h, pl.ds(((q * slabs + j) * 2 + r) * pair + k, rows_a, stride=modes_x), :][:, :wide]
                 for r in range(2) for k in range(pair)], 1)
        start(0, h * chunks + q)

    middle = packed // 2

    def first_forward(q):
        arrived(0, q)
        result = from_left(fa, r1[q])
        cosine, sine = result[:2 * half], result[2 * half:]
        result = cosine + jnp.concatenate([sine[:, middle:], -sine[:, :middle]], 1)
        s2[q] = result.reshape(s2.shape[1:])
        start(1, q)
        if q < chunks:
            send_lines(1, q)

    def second(q):
        arrived(1, q)
        blocks = []
        for kb in range(pair * few):
            blocks.append(jnp.concatenate(
                [r2[q, p, :, r * middle + kb * rows_c:r * middle + (kb + 1) * rows_c]
                 for r in range(2) for p in range(pencils)], 1))
        spectrum = from_right(jnp.concatenate(blocks, 0), fc)
        mode_k = row_k[...] + (q % chunks * slabs * pair + i_s * pair).astype(jnp.float32)
        mode_f = row_f[...] + (i_p * f_block - half).astype(jnp.float32)
        squared = mode_k * mode_k + mode_f * mode_f + col_s[...]
        radius = float(half * half)
        kinetic = jnp.where(squared < radius, 4.0 * squared / radius, 0.0) * (1.0 / float(length**3))
        result = from_right(spectrum * kinetic, ic)
        for p in range(pencils):
            s3[q, p] = jnp.concatenate(
                [result[kb * f_block:(kb + 1) * f_block, (p * 2 + r) * rows_c:(p * 2 + r + 1) * rows_c]
                 for r in range(2) for kb in range(pair * few)], 1)
        start(2, q)

    def first_inverse(q):
        arrived(2, q)
        result = from_left(ia, r3[q])
        cosine, sine = result[:length], result[length:]
        result = cosine + jnp.concatenate([-sine[:, middle:], sine[:, :middle]], 1)
        s4[q] = result.reshape(s4.shape[1:])
        start(3, q)

    def take_lines(h, q):
        arrived(3, h * chunks + q)
        unused = jnp.zeros((rows_a, 128 - wide), jnp.float32)
        for j in range(slabs):
            value = r4[h * chunks + q, j]
            for r in range(2):
                for k in range(pair):
                    piece = value[:, r * middle + k * wide:r * middle + (k + 1) * wide]
                    back[h, pl.ds(((q * slabs + j) * 2 + r) * pair + k, rows_a, stride=modes_x), :] = (
                        jnp.concatenate([piece, unused], 1))

    def inverse_x(h, first, end):
        def body(g, carry):
            spectra = []
            for n in range(group):
                at = pl.multiple_of((g * group + n) * modes_x, modes_x)
                spectra.append(back[h, pl.ds(at, modes_x), 0:wide].T)
            kinetic_parts = from_right(jnp.concatenate(spectra, 0), ix)
            for n in range(group):
                a = g * group + n
                level = potential[pl.ds(a, 1)].reshape(rows_c, length)
                filtered = [out[b, pl.ds(a, 1)].reshape(rows_c, length) for b in range(h * few)]
                for b in range(few):
                    orbital = orbitals[h * few + b, pl.ds(a, 1)].reshape(rows_c, length)
                    kinetic_part = kinetic_parts[n * wide + b * rows_c:n * wide + (b + 1) * rows_c]
                    applied = kinetic_part + level * orbital
                    value = jnp.where(unlocked[h * few + b] == 1, (applied - orbital) / 1.5, orbital)
                    out[h * few + b, pl.ds(a, 1)] = value.reshape(1, rows_c, length)
                    filtered.append(value)
                for b in range(h * few, (h + 1) * few):
                    for e in range(b + 1):
                        squares = filtered[b] * filtered[e]
                        sums[b * (b + 1) // 2 + e] += squares.reshape(rows_c // 8, 8, length).sum(0)
            return carry

        lax.fori_loop(first, end, body, 0)

    sums[...] = jnp.zeros_like(sums)
    forward_x(0)
    pl.semaphore_wait(barrier, slabs - 1 + pencils - 1)
    for q in range(chunks):
        send_lines(0, q)
    forward_x(1)
    last = 2 * chunks
    for step in range(last + 1):
        if step < last:
            first_forward(step)
        if step >= 1:
            second(step - 1)
        if step >= 2:
            first_inverse(step - 2)
        if step >= last - 1:
            for q in range(chunks - 1) if step < last else range(chunks - 1, chunks):
                take_lines(0, q)
    groups = rows_a // group
    early = groups - groups // 3
    fetch_potential.wait()
    inverse_x(0, 0, early)
    first_inverse(last - 1)
    inverse_x(0, early, groups)
    keep(0).start()
    for q in range(chunks):
        take_lines(1, q)
    inverse_x(1, 0, groups)
    keep(1).start()

    total = jnp.sum(jnp.sum(sums[...], axis=1), axis=1, keepdims=True)
    g1[...] = jnp.broadcast_to(total, g1.shape)
    shares = [to_slab(d, g1, h1.at[i_s], gs1.at[d], gr1.at[d]) for d in range(1, slabs)]
    for copy in shares:
        copy.start()
    h1[pl.ds(i_s, 1)] = g1[...][None]
    for copy in shares:
        copy.wait()
    g2[...] = jnp.sum(h1[...], axis=0)
    shares = [to_pencil(d, g2, h2.at[i_p], gs2.at[d], gr2.at[d]) for d in range(1, pencils)]
    for copy in shares:
        copy.start()
    h2[pl.ds(i_p, 1)] = g2[...][None]
    for copy in shares:
        copy.wait()
    gram = jnp.sum(h2[...], axis=0) / float(length**3)

    factor = {}
    for b in range(bands):
        for e in range(b + 1):
            n = b * (b + 1) // 2 + e
            value = gram[n:n + 1, 0:1]
            for m in range(e):
                value = value - factor[b, m] * factor[e, m]
            factor[b, e] = jnp.sqrt(value) if b == e else value / factor[e, e]
    entries = [1.0 / factor[b, e] if b == e else factor[b, e] for b in range(bands) for e in range(b + 1)]
    for n, entry in enumerate(entries):
        solver[n:n + 1, :] = jnp.broadcast_to(entry, (1, 128))
    for h in range(2):
        keep(h).wait()
    for which in range(4):
        for q in range(2 * chunks):
            for copy in copies(which, q)[0]:
                copy.wait_send()


def solve(solver, filtered, out):
    bands, rows_a, rows_c, length = filtered.shape
    for a in range(rows_a):
        solved = []
        for b in range(bands):
            value = filtered[b, a]
            first = b * (b + 1) // 2
            for m in range(b):
                value = value - solver[first + m, 0] * solved[m]
            value = value * solver[first + b, 0]
            out[b, a] = value
            solved.append(value)


def by_kernel(slabs, pencils, chunks, orbitals, potential, unlocked):
    bands, rows_a, rows_c, length = orbitals.shape
    half = length // 4
    pair = half // (slabs * chunks)
    f_block = 2 * half // pencils
    few = bands // 2
    parts = 2 * chunks
    packed = 2 * pair * few * rows_c
    pairs = bands * (bands + 1) // 2
    tables = dft_tables(length, slabs, pencils, chunks)
    rows = np.arange(pair * few * f_block)
    row_k = (rows // (few * f_block)).astype(np.float32)[:, None]
    row_f = (rows % f_block).astype(np.float32)[:, None]
    col_s = ((np.arange(4 * half) % (2 * half) - half).astype(np.float32) ** 2)[None, :]
    vmem = pl.BlockSpec(memory_space=pltpu.VMEM)
    f32 = jnp.float32
    dma = pltpu.SemaphoreType.DMA
    scratch = [
        pltpu.VMEM(orbitals.shape, f32),
        pltpu.VMEM(potential.shape, f32),
        pltpu.VMEM(orbitals.shape, f32),
        dma((3, rows_a // 8)),
        dma((2,)),
        pltpu.VMEM((2, rows_a * 2 * half, 128), f32),
        pltpu.VMEM((parts, slabs, rows_a, packed), f32),
        pltpu.VMEM((parts, length, packed), f32),
        pltpu.VMEM((parts, pencils, f_block, packed), f32),
        pltpu.VMEM((parts, pencils, f_block, packed), f32),
        pltpu.VMEM((parts, pencils, f_block, packed), f32),
        pltpu.VMEM((parts, 2 * half, packed), f32),
        pltpu.VMEM((parts, slabs, rows_a, packed), f32),
        pltpu.VMEM((parts, slabs, rows_a, packed), f32),
        pltpu.VMEM((2, rows_a * 2 * half, 128), f32),
        pltpu.VMEM((pairs, 8, length), f32),
        pltpu.VMEM((pairs, 128), f32),
        pltpu.VMEM((slabs, pairs, 128), f32),
        pltpu.VMEM((pairs, 128), f32),
        pltpu.VMEM((pencils, pairs, 128), f32),
        dma((4, parts)),
        dma((parts, slabs)), dma((parts, slabs)),
        dma((parts, pencils)), dma((parts, pencils)),
        dma((parts, pencils)), dma((parts, pencils)),
        dma((parts, slabs)), dma((parts, slabs)),
        dma((slabs,)), dma((slabs,)),
        dma((pencils,)), dma((pencils,)),
    ]
    flops = 2 * rows_a * bands * rows_c * length * 2 * half * 6
    anywhere = pl.BlockSpec(memory_space=pl.ANY)
    filtered, solver = pl.pallas_call(
        functools.partial(kernel, (slabs, pencils, chunks, pair, bands, length)),
        out_shape=[jax.ShapeDtypeStruct(orbitals.shape, f32), jax.ShapeDtypeStruct((pairs, 128), f32)],
        in_specs=[pl.BlockSpec(memory_space=pltpu.SMEM)] + [pl.BlockSpec(memory_space=pltpu.HBM)] * 2 + [vmem] * 9,
        out_specs=[anywhere, vmem],
        scratch_shapes=scratch,
        compiler_params=pltpu.CompilerParams(
            collective_id=0, has_side_effects=True, vmem_limit_bytes=36 * 1024 * 1024),
        cost_estimate=pl.CostEstimate(flops=flops, bytes_accessed=10 * 2**20, transcendentals=0),
    )(unlocked, orbitals, potential, *[jnp.asarray(t) for t in tables],
      jnp.asarray(row_k), jnp.asarray(row_f), jnp.asarray(col_s))
    planes = 8
    block = pl.BlockSpec((bands, planes, rows_c, length), lambda i: (0, i, 0, 0))
    return pl.pallas_call(
        solve,
        grid=(rows_a // planes,),
        out_shape=jax.ShapeDtypeStruct(orbitals.shape, f32),
        in_specs=[pl.BlockSpec(memory_space=pltpu.SMEM), block],
        out_specs=block,
        cost_estimate=pl.CostEstimate(flops=20 * orbitals.size, bytes_accessed=8 * orbitals.size, transcendentals=0),
    )(solver, filtered)


NG = 192


kinetic_scale = 4.0
filter_center = 1.0
filter_half = 1.5
highest = lax.Precision.HIGHEST


def frequencies(number, length):
    index = jnp.arange(number, dtype=jnp.int32)
    if number == length:
        return jnp.where(index < length // 2, index, index - length)
    return index - length // 4


def tables(number, length):
    modes = frequencies(number, length)
    places = jnp.arange(length, dtype=jnp.int32)
    product = places[:, None] * modes[None, :] % length
    angle = 2.0 * math.pi / length * product.astype(jnp.float32)
    return (jnp.cos(angle), jnp.sin(angle))


def forward_table(cosine, sine):
    return jnp.stack([jnp.stack([cosine, -sine], 1), jnp.stack([sine, cosine], 1)], 1)


def inverse_table(cosine, sine):
    cos_t = cosine.T
    sin_t = sine.T
    return jnp.stack([jnp.stack([cos_t, sin_t], 1), jnp.stack([-sin_t, cos_t], 1)], 1)


def by_collectives(orbitals, potential, unlocked):
    length = orbitals.shape[3]
    kept_modes = length // 2
    cos_k, sin_k = tables(kept_modes, length)
    cos_f, sin_f = tables(length, length)
    first_forward = jnp.stack([cos_k, -sin_k], 1)
    first_inverse = jnp.stack([cos_k.T, -sin_k.T], 1)
    second_forward = forward_table(cos_k, sin_k)
    second_inverse = inverse_table(cos_k, sin_k)
    depth_forward = forward_table(cos_f, sin_f)
    depth_inverse = inverse_table(cos_f, sin_f)
    pencil_block = kept_modes // lax.axis_size("pencil")
    slab_block = kept_modes // lax.axis_size("slab")
    kept_list = frequencies(kept_modes, length)
    third_modes = lax.dynamic_slice_in_dim(
        kept_list, lax.axis_index("pencil") * pencil_block, pencil_block
    ).astype(jnp.float32)
    second_modes = lax.dynamic_slice_in_dim(
        kept_list, lax.axis_index("slab") * slab_block, slab_block
    ).astype(jnp.float32)
    first_modes = frequencies(length, length).astype(jnp.float32)
    squared = (
        third_modes[:, None, None] ** 2
        + second_modes[None, :, None] ** 2
        + first_modes[None, None, :] ** 2
    )
    radius = float((length // 4) ** 2)
    kinetic = jnp.where(squared < radius, kinetic_scale * squared / radius, 0.0)
    lines_k = jnp.einsum("bacx,xrk->bacrk", orbitals, first_forward, precision=highest)
    along_f = jnp.einsum(
        "bacrk,crsf->baksf",
        lax.all_to_all(lines_k, "pencil", split_axis=4, concat_axis=2, tiled=True),
        second_forward,
        precision=highest,
    )
    spectra = jnp.einsum(
        "baksf,astg->bkftg",
        lax.all_to_all(along_f, "slab", split_axis=4, concat_axis=1, tiled=True),
        depth_forward,
        precision=highest,
    )
    spectra = spectra * kinetic[None, :, :, None, :]
    along_a = jnp.einsum("bkftg,gtsa->bkfsa", spectra, depth_inverse, precision=highest)
    returned = lax.all_to_all(along_a, "slab", split_axis=4, concat_axis=2, tiled=True)
    rows_c = jnp.einsum("bkfsa,fsrc->bkarc", returned, second_inverse, precision=highest)
    lines_x = lax.all_to_all(rows_c, "pencil", split_axis=4, concat_axis=1, tiled=True)
    kinetic_part = jnp.einsum("bkarc,krx->bacx", lines_x, first_inverse, precision=highest)
    kinetic_part = kinetic_part / float(NG**3)
    applied = kinetic_part + potential[None] * orbitals
    filtered = jnp.where(
        unlocked[:, None, None, None] == 1,
        (applied - filter_center * orbitals) / filter_half,
        orbitals,
    )
    number = filtered.shape[0]
    flattened = filtered.reshape(number, -1)
    partial_intersection = jnp.dot(flattened, flattened.T, precision=highest) / float(NG**3)
    intersection = lax.psum(partial_intersection, ("slab", "pencil"))
    factor = jnp.linalg.cholesky(intersection)
    result = jax.scipy.linalg.solve_triangular(factor, flattened, lower=True)
    return result.reshape(filtered.shape)


def solution(mesh):
    slabs, pencils = mesh.shape["slab"], mesh.shape["pencil"]

    def local(orbitals, potential, unlocked):
        bands, rows_a, rows_c, length = orbitals.shape
        half = length // 4
        f_block = 2 * half // pencils
        chunks = half // (2 * slabs)
        even = bands % 2 == 0 and bands // 2 * rows_c <= 128 and chunks > 0 and half % (2 * slabs) == 0
        fits = even and rows_a % 8 == 0 and rows_c % 8 == 0 and f_block % 8 == 0
        if fits:
            return by_kernel(slabs, pencils, chunks, orbitals, potential, unlocked)
        return by_collectives(orbitals, potential, unlocked)

    in_specs = (P(None, "slab", "pencil", None), P("slab", "pencil", None), P())
    out_specs = P(None, "slab", "pencil", None)
    return jax.shard_map(local, mesh=mesh, in_specs=in_specs, out_specs=out_specs, check_vma=False)
```

```python
import functools
import math

import jax
import jax.numpy as jnp
import ml_dtypes
import numpy as np
from jax import lax
from jax.experimental import pallas as pl
from jax.experimental.pallas import tpu as pltpu
from jax.sharding import PartitionSpec as P

MESH = pl.DeviceIdType.MESH


def dft_tables(length, slabs, pencils, chunks):
    half = length // 4
    pair = half // (slabs * chunks)
    place = np.arange(length)
    modes = np.arange(2 * half) - half
    third = np.arange(half)

    def waves(mode):
        angle = 2.0 * np.pi / length * ((mode[:, None] * place[None, :]) % length)
        return np.cos(angle), np.sin(angle)

    cos_k, sin_k = waves(third)
    weight = np.where(third == 0, 1.0, 2.0)[:, None]

    def order(cosine, sine):
        both = np.stack([cosine, sine], 0).reshape(2, chunks, slabs, pair, length)
        return both.transpose(1, 2, 0, 3, 4).reshape(2 * half, length)

    forward_x = order(cos_k, -sin_k).T
    inverse_x = order(weight * cos_k, -weight * sin_k)
    cosine, sine = waves(modes)
    forward = np.stack([np.stack([cosine, sine], 1), np.stack([-sine, cosine], 1)], 0)
    inverse = np.stack([np.stack([cosine.T, -sine.T], 1), np.stack([sine.T, cosine.T], 1)], 0)
    c_block = length // pencils
    forward_a = np.concatenate([cosine, sine], 0)
    forward_c = forward.reshape(4 * half, 2 * length).T
    inverse_c = inverse.reshape(2, pencils, c_block, 4 * half).transpose(1, 0, 2, 3).reshape(2 * length, 4 * half).T
    inverse_a = np.concatenate([cosine.T, sine.T], 0)
    tables = (forward_x, forward_a, forward_c, inverse_c, inverse_a, inverse_x)
    pairs = []
    for table in tables:
        high = table.astype(ml_dtypes.bfloat16)
        low = (table - high.astype(np.float64)).astype(ml_dtypes.bfloat16)
        pairs.append(np.stack([high, low], 0))
    return pairs


def split(value):
    high = value.astype(jnp.bfloat16)
    return high, (value - high.astype(jnp.float32)).astype(jnp.bfloat16)


def product(left, right):
    return jnp.dot(left, right, preferred_element_type=jnp.float32)


def from_left(table, value):
    high, low = split(value)
    return product(table[0], high) + (product(table[0], low) + product(table[1], high))


def from_right(value, table):
    high, low = split(value)
    return product(high, table[0]) + (product(low, table[0]) + product(high, table[1]))


def kernel(sizes, unlocked, given, given_potential, *rest):
    given_tables, (kept, solver), tables, rest = rest[:9], rest[9:11], rest[11:20], rest[20:]
    fx, fa, fc, ic, ia, ix, row_k, row_f, col_s = tables
    (orbitals, potential, out, load, store, load_tables, lines, s1, r1, s2, r2, s3, r3, s4, r4, back, sums, g1, h1, g2, h2,
           own, send1, recv1, send2, recv2, send3, recv3, send4, recv4, gs1, gr1, gs2, gr2) = rest
    slabs, pencils, chunks, pair, bands, length = sizes
    few = bands // 2
    rows_a = orbitals.shape[1]
    rows_c = orbitals.shape[2]
    half = length // 4
    f_block = 2 * half // pencils
    wide = few * rows_c
    packed = 2 * pair * wide
    i_s = lax.axis_index("slab")
    i_p = lax.axis_index("pencil")

    def slab_peer(d):
        return lax.rem(i_s + d, slabs)

    def pencil_peer(d):
        return lax.rem(i_p + d, pencils)

    group = 8

    def fetch(h, g):
        at = (pl.ds(h * few, few), pl.ds(pl.multiple_of(g * group, group), group))
        return pltpu.make_async_copy(given.at[at], orbitals.at[at], load.at[h, g])

    fetch_tables = [pltpu.make_async_copy(src, dst, load_tables.at[n])
                    for n, (src, dst) in enumerate(zip(given_tables, tables))]
    fetch_tables[0].start()
    fetch_potential = pltpu.make_async_copy(given_potential, potential, load.at[2, 0])
    for h in range(2):
        for g in range(rows_a // group):
            fetch(h, g).start()
    for copy in fetch_tables[1:]:
        copy.start()
    fetch_potential.start()

    def keep(h):
        return pltpu.make_async_copy(out.at[pl.ds(h * few, few)], kept.at[pl.ds(h * few, few)], store.at[h])

    barrier = pltpu.get_barrier_semaphore()
    for d in range(1, slabs):
        pl.semaphore_signal(barrier, inc=1, device_id=(slab_peer(d), i_p), device_id_type=MESH)
    for d in range(1, pencils):
        pl.semaphore_signal(barrier, inc=1, device_id=(i_s, pencil_peer(d)), device_id_type=MESH)

    def to_slab(d, src, dst, send, recv):
        return pltpu.make_async_remote_copy(
            src_ref=src, dst_ref=dst, send_sem=send, recv_sem=recv,
            device_id=(slab_peer(d), i_p), device_id_type=MESH)

    def to_pencil(d, src, dst, send, recv):
        return pltpu.make_async_remote_copy(
            src_ref=src, dst_ref=dst, send_sem=send, recv_sem=recv,
            device_id=(i_s, pencil_peer(d)), device_id_type=MESH)

    mine_a = pl.ds(pl.multiple_of(i_s * rows_a, 8), rows_a)
    mine_f = pl.ds(pl.multiple_of(i_p * f_block, 8), f_block)

    def copies(which, q):
        if which == 0:
            remote = [to_slab(d, s1.at[q, slab_peer(d)], r1.at[q, mine_a, :], send1.at[q, d], recv1.at[q, d])
                      for d in range(1, slabs)]
            local = pltpu.make_async_copy(s1.at[q, i_s], r1.at[q, mine_a, :], own.at[0, q])
        elif which == 1:
            remote = [to_pencil(d, s2.at[q, pencil_peer(d)], r2.at[q, i_p], send2.at[q, d], recv2.at[q, d])
                      for d in range(1, pencils)]
            local = pltpu.make_async_copy(s2.at[q, i_p], r2.at[q, i_p], own.at[1, q])
        elif which == 2:
            remote = [to_pencil(d, s3.at[q, pencil_peer(d)], r3.at[q, mine_f, :], send3.at[q, d], recv3.at[q, d])
                      for d in range(1, pencils)]
            local = pltpu.make_async_copy(s3.at[q, i_p], r3.at[q, mine_f, :], own.at[2, q])
        else:
            remote = [to_slab(d, s4.at[q, slab_peer(d)], r4.at[q, i_s], send4.at[q, d], recv4.at[q, d])
                      for d in range(1, slabs)]
            local = pltpu.make_async_copy(s4.at[q, i_s], r4.at[q, i_s], own.at[3, q])
        return remote, local

    def start(which, q):
        remote, local = copies(which, q)
        for copy in remote:
            copy.start()
        local.start()

    def arrived(which, q):
        remote, local = copies(which, q)
        for copy in remote:
            copy.wait_recv()
        local.wait()

    modes_x = 2 * half

    def forward_x(h):
        def body(g, carry):
            fetch(h, g).wait()
            rows = jnp.concatenate(
                [orbitals[h * few:(h + 1) * few, pl.ds(g * group + n, 1)].reshape(wide, length)
                 for n in range(group)], 0)
            result = from_right(rows, fx)
            for n in range(group):
                at = pl.multiple_of((g * group + n) * modes_x, modes_x)
                lines[h, pl.ds(at, modes_x), 0:wide] = result[n * wide:(n + 1) * wide].T
            return carry

        lax.fori_loop(0, rows_a // group, body, 0)

    def send_lines(h, q):
        for j in range(slabs):
            s1[h * chunks + q, j] = jnp.concatenate(
                [lines[h, pl.ds(((q * slabs + j) * 2 + r) * pair + k, rows_a, stride=modes_x), :][:, :wide]
                 for r in range(2) for k in range(pair)], 1)
        start(0, h * chunks + q)

    middle = packed // 2

    def first_forward(q):
        arrived(0, q)
        result = from_left(fa, r1[q])
        cosine, sine = result[:2 * half], result[2 * half:]
        result = cosine + jnp.concatenate([sine[:, middle:], -sine[:, :middle]], 1)
        s2[q] = result.reshape(s2.shape[1:])
        start(1, q)
        if q < chunks:
            send_lines(1, q)

    def second(q):
        arrived(1, q)
        blocks = []
        for kb in range(pair * few):
            blocks.append(jnp.concatenate(
                [r2[q, p, :, r * middle + kb * rows_c:r * middle + (kb + 1) * rows_c]
                 for r in range(2) for p in range(pencils)], 1))
        spectrum = from_right(jnp.concatenate(blocks, 0), fc)
        mode_k = row_k[...] + (q % chunks * slabs * pair + i_s * pair).astype(jnp.float32)
        mode_f = row_f[...] + (i_p * f_block - half).astype(jnp.float32)
        squared = mode_k * mode_k + mode_f * mode_f + col_s[...]
        radius = float(half * half)
        kinetic = jnp.where(squared < radius, 4.0 * squared / radius, 0.0) * (1.0 / float(length**3))
        result = from_right(spectrum * kinetic, ic)
        for p in range(pencils):
            s3[q, p] = jnp.concatenate(
                [result[kb * f_block:(kb + 1) * f_block, (p * 2 + r) * rows_c:(p * 2 + r + 1) * rows_c]
                 for r in range(2) for kb in range(pair * few)], 1)
        start(2, q)

    def first_inverse(q):
        arrived(2, q)
        result = from_left(ia, r3[q])
        cosine, sine = result[:length], result[length:]
        result = cosine + jnp.concatenate([-sine[:, middle:], sine[:, :middle]], 1)
        s4[q] = result.reshape(s4.shape[1:])
        start(3, q)

    def take_lines(h, q):
        arrived(3, h * chunks + q)
        unused = jnp.zeros((rows_a, 128 - wide), jnp.float32)
        for j in range(slabs):
            value = r4[h * chunks + q, j]
            for r in range(2):
                for k in range(pair):
                    piece = value[:, r * middle + k * wide:r * middle + (k + 1) * wide]
                    back[h, pl.ds(((q * slabs + j) * 2 + r) * pair + k, rows_a, stride=modes_x), :] = (
                        jnp.concatenate([piece, unused], 1))

    def inverse_x(h, first, end):
        def body(g, carry):
            spectra = []
            for n in range(group):
                at = pl.multiple_of((g * group + n) * modes_x, modes_x)
                spectra.append(back[h, pl.ds(at, modes_x), 0:wide].T)
            kinetic_parts = from_right(jnp.concatenate(spectra, 0), ix)
            for n in range(group):
                a = g * group + n
                level = potential[pl.ds(a, 1)].reshape(rows_c, length)
                filtered = [out[b, pl.ds(a, 1)].reshape(rows_c, length) for b in range(h * few)]
                for b in range(few):
                    orbital = orbitals[h * few + b, pl.ds(a, 1)].reshape(rows_c, length)
                    kinetic_part = kinetic_parts[n * wide + b * rows_c:n * wide + (b + 1) * rows_c]
                    applied = kinetic_part + level * orbital
                    value = jnp.where(unlocked[h * few + b] == 1, (applied - orbital) / 1.5, orbital)
                    out[h * few + b, pl.ds(a, 1)] = value.reshape(1, rows_c, length)
                    filtered.append(value)
                for b in range(h * few, (h + 1) * few):
                    for e in range(b + 1):
                        squares = filtered[b] * filtered[e]
                        sums[b * (b + 1) // 2 + e] += squares.reshape(rows_c // 8, 8, length).sum(0)
            return carry

        lax.fori_loop(first, end, body, 0)

    sums[...] = jnp.zeros_like(sums)
    fetch_tables[0].wait()
    forward_x(0)
    pl.semaphore_wait(barrier, slabs - 1 + pencils - 1)
    for q in range(chunks):
        send_lines(0, q)
    forward_x(1)
    for copy in fetch_tables[1:]:
        copy.wait()
    last = 2 * chunks
    for step in range(last + 1):
        if step < last:
            first_forward(step)
        if step >= 1:
            second(step - 1)
        if step >= 2:
            first_inverse(step - 2)
        if step >= last - 1:
            for q in range(chunks - 1) if step < last else range(chunks - 1, chunks):
                take_lines(0, q)
    groups = rows_a // group
    early = groups - groups // 3
    fetch_potential.wait()
    inverse_x(0, 0, early)
    first_inverse(last - 1)
    inverse_x(0, early, groups)
    keep(0).start()
    for q in range(chunks):
        take_lines(1, q)
    inverse_x(1, 0, groups)
    keep(1).start()

    total = jnp.sum(jnp.sum(sums[...], axis=1), axis=1, keepdims=True)
    g1[...] = jnp.broadcast_to(total, g1.shape)
    shares = [to_slab(d, g1, h1.at[i_s], gs1.at[d], gr1.at[d]) for d in range(1, slabs)]
    for copy in shares:
        copy.start()
    h1[pl.ds(i_s, 1)] = g1[...][None]
    for copy in shares:
        copy.wait()
    g2[...] = jnp.sum(h1[...], axis=0)
    shares = [to_pencil(d, g2, h2.at[i_p], gs2.at[d], gr2.at[d]) for d in range(1, pencils)]
    for copy in shares:
        copy.start()
    h2[pl.ds(i_p, 1)] = g2[...][None]
    for copy in shares:
        copy.wait()
    gram = jnp.sum(h2[...], axis=0) / float(length**3)

    factor = {}
    for b in range(bands):
        for e in range(b + 1):
            n = b * (b + 1) // 2 + e
            value = gram[n:n + 1, 0:1]
            for m in range(e):
                value = value - factor[b, m] * factor[e, m]
            factor[b, e] = jnp.sqrt(value) if b == e else value / factor[e, e]
    entries = [1.0 / factor[b, e] if b == e else factor[b, e] for b in range(bands) for e in range(b + 1)]
    for n, entry in enumerate(entries):
        solver[n:n + 1, :] = jnp.broadcast_to(entry, (1, 128))
    for h in range(2):
        keep(h).wait()
    for which in range(4):
        for q in range(2 * chunks):
            for copy in copies(which, q)[0]:
                copy.wait_send()


def solve(solver, filtered, out):
    bands, rows_a, rows_c, length = filtered.shape
    for a in range(rows_a):
        solved = []
        for b in range(bands):
            value = filtered[b, a]
            first = b * (b + 1) // 2
            for m in range(b):
                value = value - solver[first + m, 0] * solved[m]
            value = value * solver[first + b, 0]
            out[b, a] = value
            solved.append(value)


def by_kernel(slabs, pencils, chunks, orbitals, potential, unlocked):
    bands, rows_a, rows_c, length = orbitals.shape
    half = length // 4
    pair = half // (slabs * chunks)
    f_block = 2 * half // pencils
    few = bands // 2
    parts = 2 * chunks
    packed = 2 * pair * few * rows_c
    pairs = bands * (bands + 1) // 2
    tables = dft_tables(length, slabs, pencils, chunks)
    rows = np.arange(pair * few * f_block)
    row_k = (rows // (few * f_block)).astype(np.float32)[:, None]
    row_f = (rows % f_block).astype(np.float32)[:, None]
    col_s = ((np.arange(4 * half) % (2 * half) - half).astype(np.float32) ** 2)[None, :]
    vmem = pl.BlockSpec(memory_space=pltpu.VMEM)
    f32 = jnp.float32
    dma = pltpu.SemaphoreType.DMA
    given = tables + [row_k, row_f, col_s]
    scratch = [pltpu.VMEM(t.shape, t.dtype) for t in given] + [
        pltpu.VMEM(orbitals.shape, f32),
        pltpu.VMEM(potential.shape, f32),
        pltpu.VMEM(orbitals.shape, f32),
        dma((3, rows_a // 8)),
        dma((2,)),
        dma((9,)),
        pltpu.VMEM((2, rows_a * 2 * half, 128), f32),
        pltpu.VMEM((parts, slabs, rows_a, packed), f32),
        pltpu.VMEM((parts, length, packed), f32),
        pltpu.VMEM((parts, pencils, f_block, packed), f32),
        pltpu.VMEM((parts, pencils, f_block, packed), f32),
        pltpu.VMEM((parts, pencils, f_block, packed), f32),
        pltpu.VMEM((parts, 2 * half, packed), f32),
        pltpu.VMEM((parts, slabs, rows_a, packed), f32),
        pltpu.VMEM((parts, slabs, rows_a, packed), f32),
        pltpu.VMEM((2, rows_a * 2 * half, 128), f32),
        pltpu.VMEM((pairs, 8, length), f32),
        pltpu.VMEM((pairs, 128), f32),
        pltpu.VMEM((slabs, pairs, 128), f32),
        pltpu.VMEM((pairs, 128), f32),
        pltpu.VMEM((pencils, pairs, 128), f32),
        dma((4, parts)),
        dma((parts, slabs)), dma((parts, slabs)),
        dma((parts, pencils)), dma((parts, pencils)),
        dma((parts, pencils)), dma((parts, pencils)),
        dma((parts, slabs)), dma((parts, slabs)),
        dma((slabs,)), dma((slabs,)),
        dma((pencils,)), dma((pencils,)),
    ]
    flops = 2 * rows_a * bands * rows_c * length * 2 * half * 6
    anywhere = pl.BlockSpec(memory_space=pl.ANY)
    filtered, solver = pl.pallas_call(
        functools.partial(kernel, (slabs, pencils, chunks, pair, bands, length)),
        out_shape=[jax.ShapeDtypeStruct(orbitals.shape, f32), jax.ShapeDtypeStruct((pairs, 128), f32)],
        in_specs=[pl.BlockSpec(memory_space=pltpu.SMEM), anywhere, anywhere] + [anywhere] * 9,
        out_specs=[anywhere, vmem],
        scratch_shapes=scratch,
        compiler_params=pltpu.CompilerParams(
            collective_id=0, has_side_effects=True, vmem_limit_bytes=56 * 1024 * 1024),
        cost_estimate=pl.CostEstimate(flops=flops, bytes_accessed=10 * 2**20, transcendentals=0),
    )(unlocked, orbitals, potential, *[jnp.asarray(t) for t in given])
    planes = 8
    block = pl.BlockSpec((bands, planes, rows_c, length), lambda i: (0, i, 0, 0))
    return pl.pallas_call(
        solve,
        grid=(rows_a // planes,),
        out_shape=jax.ShapeDtypeStruct(orbitals.shape, f32),
        in_specs=[pl.BlockSpec(memory_space=pltpu.SMEM), block],
        out_specs=block,
        cost_estimate=pl.CostEstimate(flops=20 * orbitals.size, bytes_accessed=8 * orbitals.size, transcendentals=0),
    )(solver, filtered)


NG = 192


kinetic_scale = 4.0
filter_center = 1.0
filter_half = 1.5
highest = lax.Precision.HIGHEST


def frequencies(number, length):
    index = jnp.arange(number, dtype=jnp.int32)
    if number == length:
        return jnp.where(index < length // 2, index, index - length)
    return index - length // 4


def tables(number, length):
    modes = frequencies(number, length)
    places = jnp.arange(length, dtype=jnp.int32)
    product = places[:, None] * modes[None, :] % length
    angle = 2.0 * math.pi / length * product.astype(jnp.float32)
    return (jnp.cos(angle), jnp.sin(angle))


def forward_table(cosine, sine):
    return jnp.stack([jnp.stack([cosine, -sine], 1), jnp.stack([sine, cosine], 1)], 1)


def inverse_table(cosine, sine):
    cos_t = cosine.T
    sin_t = sine.T
    return jnp.stack([jnp.stack([cos_t, sin_t], 1), jnp.stack([-sin_t, cos_t], 1)], 1)


def by_collectives(orbitals, potential, unlocked):
    length = orbitals.shape[3]
    kept_modes = length // 2
    cos_k, sin_k = tables(kept_modes, length)
    cos_f, sin_f = tables(length, length)
    first_forward = jnp.stack([cos_k, -sin_k], 1)
    first_inverse = jnp.stack([cos_k.T, -sin_k.T], 1)
    second_forward = forward_table(cos_k, sin_k)
    second_inverse = inverse_table(cos_k, sin_k)
    depth_forward = forward_table(cos_f, sin_f)
    depth_inverse = inverse_table(cos_f, sin_f)
    pencil_block = kept_modes // lax.axis_size("pencil")
    slab_block = kept_modes // lax.axis_size("slab")
    kept_list = frequencies(kept_modes, length)
    third_modes = lax.dynamic_slice_in_dim(
        kept_list, lax.axis_index("pencil") * pencil_block, pencil_block
    ).astype(jnp.float32)
    second_modes = lax.dynamic_slice_in_dim(
        kept_list, lax.axis_index("slab") * slab_block, slab_block
    ).astype(jnp.float32)
    first_modes = frequencies(length, length).astype(jnp.float32)
    squared = (
        third_modes[:, None, None] ** 2
        + second_modes[None, :, None] ** 2
        + first_modes[None, None, :] ** 2
    )
    radius = float((length // 4) ** 2)
    kinetic = jnp.where(squared < radius, kinetic_scale * squared / radius, 0.0)
    lines_k = jnp.einsum("bacx,xrk->bacrk", orbitals, first_forward, precision=highest)
    along_f = jnp.einsum(
        "bacrk,crsf->baksf",
        lax.all_to_all(lines_k, "pencil", split_axis=4, concat_axis=2, tiled=True),
        second_forward,
        precision=highest,
    )
    spectra = jnp.einsum(
        "baksf,astg->bkftg",
        lax.all_to_all(along_f, "slab", split_axis=4, concat_axis=1, tiled=True),
        depth_forward,
        precision=highest,
    )
    spectra = spectra * kinetic[None, :, :, None, :]
    along_a = jnp.einsum("bkftg,gtsa->bkfsa", spectra, depth_inverse, precision=highest)
    returned = lax.all_to_all(along_a, "slab", split_axis=4, concat_axis=2, tiled=True)
    rows_c = jnp.einsum("bkfsa,fsrc->bkarc", returned, second_inverse, precision=highest)
    lines_x = lax.all_to_all(rows_c, "pencil", split_axis=4, concat_axis=1, tiled=True)
    kinetic_part = jnp.einsum("bkarc,krx->bacx", lines_x, first_inverse, precision=highest)
    kinetic_part = kinetic_part / float(NG**3)
    applied = kinetic_part + potential[None] * orbitals
    filtered = jnp.where(
        unlocked[:, None, None, None] == 1,
        (applied - filter_center * orbitals) / filter_half,
        orbitals,
    )
    number = filtered.shape[0]
    flattened = filtered.reshape(number, -1)
    partial_intersection = jnp.dot(flattened, flattened.T, precision=highest) / float(NG**3)
    intersection = lax.psum(partial_intersection, ("slab", "pencil"))
    factor = jnp.linalg.cholesky(intersection)
    result = jax.scipy.linalg.solve_triangular(factor, flattened, lower=True)
    return result.reshape(filtered.shape)


def solution(mesh):
    slabs, pencils = mesh.shape["slab"], mesh.shape["pencil"]

    def local(orbitals, potential, unlocked):
        bands, rows_a, rows_c, length = orbitals.shape
        half = length // 4
        f_block = 2 * half // pencils
        chunks = half // (2 * slabs)
        even = bands % 2 == 0 and bands // 2 * rows_c <= 128 and chunks > 0 and half % (2 * slabs) == 0
        fits = even and rows_a % 8 == 0 and rows_c % 8 == 0 and f_block % 8 == 0
        if fits:
            return by_kernel(slabs, pencils, chunks, orbitals, potential, unlocked)
        return by_collectives(orbitals, potential, unlocked)

    in_specs = (P(None, "slab", "pencil", None), P("slab", "pencil", None), P())
    out_specs = P(None, "slab", "pencil", None)
    return jax.shard_map(local, mesh=mesh, in_specs=in_specs, out_specs=out_specs, check_vma=False)
```
